256 devices in a mesh: table: 32 (over z, x), dp: 8 (over y, core).
Axes of the slice: x: 4, y: 4, z: 8, core: 2. Of those that a mesh axis runs over, the one named last changes fastest.
Arguments:
- table_rows: bfloat16 [65536, 512], P('table'), may hold values from -6 to 6
- item_shard: int32 [8, 8192, 1], P('dp', 'table'), may hold values from 0 to 31; in each aligned block of 256 rows (0 to 255, 256 to 511, ..., all dimensions but the last counted through in order) at most 16 rows name the same one
- item_slot: int32 [8, 8192], P('dp', 'table'), may hold values from 0 to 2047
- seq_lengths: int32 [8, 32, 4], P('dp', 'table'), may hold values from 1 to 128, 256 in all within a row
- cotangent: bfloat16 [8, 8192, 512], P('dp', 'table'), may hold values from -6 to 6
- w_proj: bfloat16 [512, 2048], replicated, may hold values from -0.25 to 0.25
- w_out: bfloat16 [512, 512], replicated, may hold values from -0.25 to 0.25
- norm_gain: float32 [512], replicated, may hold values from 0.5 to 1.5
Outputs:
- layer_out: bfloat16 [8, 8192, 512], P('dp', 'table')
- table_grad: float32 [65536, 512], P(('table', 'dp'))
- step_proj: bfloat16 [512, 2048], replicated
- step_out: bfloat16 [512, 512], replicated
- step_gain: float32 [512], replicated
The draws below stay inside these ranges and needn't reach their ends.
Inputs may be any that keep to these rules, and one draw needn't show every extreme that they name: `item_shard`: among the 256 tokens of one pack no table shard is named by more than 16 tokens, a bound that some block reaches. `seq_lengths`: the 4 lengths of one pack sum to 256; each pack has one sequence of length 128.
All inputs are finite; a program needn't handle non-finite values.
Results may differ from the reference program's by a relative error of at most 0.015.
Values may be sent and summed in bfloat16 or wider, within the bound.
No kernel may reach another device: no remote copies, remote signals or barrier semaphores. Data moves between devices by JAX's collectives and lax.ppermute only.
A program may use at most 64 MiB of HBM per device.

```python
import math
import jax
import jax.numpy as jnp
import numpy as np
from jax import lax

D = 512
HEADS = 4
HEAD_DIM = 128
TOK_DEV = 256
ROWS_DEV = 2048
LMAX = 128
SLOTS = 4
CAP = 16
TOKENS_G = 8192
VOCAB = 65536
N_TABLE = 32
N_DP = 8


def plant(drawn, rng, least, top_value):
    longest = drawn.shape.index(max(drawn.shape))
    spots = []
    for shift in (0, 1):
        where = [jax.random.randint(jax.random.fold_in(rng, axis), (), 0, length) for axis, length in enumerate(drawn.shape)]
        where[longest] = (where[longest] + shift) % drawn.shape[longest]
        spots.append(tuple(where))
    return drawn.at[spots[0]].set(least).at[spots[1]].set(top_value)


def block_scale(rng, dims, shards, low, high):
    factor_of = 1.0
    for axis_at, parts in shards:
        draws = jax.random.uniform(jax.random.fold_in(jax.random.fold_in(rng, 6), axis_at), (parts,), jnp.float32, low / len(shards), high / len(shards))
        factor_of = factor_of * jnp.repeat(jnp.exp(draws), dims[axis_at] // parts).reshape((-1,) + (1,) * (len(dims) - 1 - axis_at))
    return factor_of


def rank_table(count, slope):
    loads = [(1 << 20) // math.isqrt(grade ** slope) + 1 for grade in range(1, count + 1)]
    spread = 1 + sum(loads) // (1 << 30)
    return np.cumsum(np.array([max(1, weight // spread) for weight in loads]))


def ranked(rng, dims, count, skew):
    listing = rank_table(count, skew)
    lot = jax.random.randint(jax.random.fold_in(rng, 1), dims, 0, int(listing[count - 1]))
    rank = jnp.searchsorted(jnp.asarray(listing, jnp.int32), lot, side="right")
    return jax.random.permutation(jax.random.fold_in(rng, 2), count)[rank].astype(jnp.int32)


def length_profile(number_of, total, bound, lean):
    loads = [(1 << 20) // math.isqrt(grade ** lean) + 1 for grade in range(2, number_of + 1)]
    rest, holding = total - bound - (number_of - 1), [1] * (number_of - 1)
    while rest > 0:
        candidates = [i for i in range(number_of - 1) if holding[i] < bound]
        whole, budget = sum([loads[i] for i in candidates]), rest
        for i in candidates:
            extra = min(bound - holding[i], max(1, budget * loads[i] // whole), rest)
            holding[i] = holding[i] + extra
            rest = rest - extra
    return np.array([bound] + holding)


def uneven(key, count, total, bound, slope):
    if count == 2:
        one = jax.random.randint(key, (), max(1, total - bound), min(bound, total - 1) + 1)
        return jnp.stack([one, total - one])
    tallies = jnp.asarray(length_profile(count, total, bound, slope), jnp.int32)
    couples = (count - 1) // 2
    source_of, sink = tallies[1:1 + 2 * couples:2], tallies[2:2 + 2 * couples:2]
    margin = jnp.minimum(source_of - 1, bound - sink)
    shifted = jax.random.randint(jax.random.fold_in(key, 1), (couples,), 0, 1 << 20) % (margin + 1)
    tallies = tallies.at[1:1 + 2 * couples:2].set(source_of - shifted).at[2:2 + 2 * couples:2].set(sink + shifted)
    return tallies[jax.random.permutation(jax.random.fold_in(key, 2), count)]


def deal_out(own_key, own, number, rows, amount, top, bound, lean):
    order = jax.random.permutation(own_key, amount)
    packed, common = portions_of(amount, rows * top, bound, lean, True), portions_of(amount, rows * top, bound, lean, False)
    places = jnp.arange(amount)

    def named(tallies, rotation):
        used = int((tallies > 0).sum())
        fixed = max(1, used // 4)
        passed = fixed + (places - fixed + rotation * (used - fixed)) % max(1, amount - fixed)
        return jnp.zeros((amount,), jnp.int32).at[order[jnp.where(places < fixed, places, passed)]].set(jnp.asarray(tallies, jnp.int32))

    tallies = jnp.where(number % 4 == 0, named(packed, number // 4), named(common, number - number // 4 - 1))
    mixed = jax.random.permutation(jax.random.fold_in(own, 3), amount)
    giver, taker = mixed[0:amount // 2 * 2:2], mixed[1:amount // 2 * 2:2]
    margin = jnp.minimum(tallies[giver] - 1, bound - tallies[taker]) // 2
    margin = jnp.where((giver == order[0]) | (taker == order[0]) | (tallies[taker] == 0), 0, jnp.maximum(margin, 0))
    passed = jax.random.randint(jax.random.fold_in(own, 4), (amount // 2,), 0, 1 << 20) % (margin + 1)
    tallies = tallies.at[giver].add(-passed).at[taker].add(passed)
    items = jnp.searchsorted(jnp.cumsum(tallies), jnp.arange(rows * top), side="right").astype(jnp.int32)
    table = items.reshape(top, rows).T
    table = table[jax.random.permutation(jax.random.fold_in(own, 1), rows)]
    rotation = jax.random.randint(jax.random.fold_in(own, 2), (rows, 1), 0, top)
    return jnp.take_along_axis(table, (jnp.arange(top)[None, :] + rotation) % top, axis=1)


def portions_of(count, total, bound, lean, full):
    loads = [(1 << 20) // math.isqrt(standing ** lean) + 1 for standing in range(1, count + 1)]
    largest = bound if full else min(bound, max(-(-total // count), total * loads[0] // sum(loads)))
    least = 1 if total - largest >= count - 1 else 0
    holding, surplus = [largest] + [least] * (count - 1), total - largest - least * (count - 1)
    while surplus > 0:
        free = [i for i in range(1, count) if holding[i] < largest] or [i for i in range(1, count) if holding[i] < bound]
        mass, remaining = sum([loads[i] for i in free]), surplus
        for i in free:
            more = min(bound - holding[i], max(1, remaining * loads[i] // mass), surplus)
            holding[i] = holding[i] + more
            surplus = surplus - more
    return np.array(holding)


def gaussian(own_key, extent, spread, bound, pieces=(), kind=jnp.bfloat16):
    result = jax.random.normal(own_key, extent, jnp.float32) * spread
    if len(pieces) > 0:
        result = block_scale(own_key, extent, pieces, -0.22, 0.18) * result
    return jnp.clip(result, min=-bound, max=bound).astype(kind)


def setup_inputs(seed: int = 0) -> dict:
    key_of = jax.random.split(jax.random.key(seed), 9)
    table_rows = gaussian(key_of[0], (VOCAB, D), 1.0, 6.0, ((0, 32),))
    item_shard_keys = jax.random.split(jax.random.fold_in(key_of[1], 1), N_DP * TOKENS_G // TOK_DEV)
    item_shard_turns = jax.random.permutation(jax.random.fold_in(key_of[1], 3), N_DP * TOKENS_G // TOK_DEV)
    item_shard = jax.vmap(lambda own, number: deal_out(jax.random.fold_in(key_of[1], 2), own, number, TOK_DEV, N_TABLE, 1, CAP, 2))(item_shard_keys, item_shard_turns).reshape((N_DP, TOKENS_G, 1))
    item_slot = plant(ranked(key_of[2], (N_DP, TOKENS_G), ROWS_DEV, 2), jax.random.fold_in(key_of[2], 3), 0, ROWS_DEV - 1).astype(jnp.int32)
    seq_lengths = jax.vmap(lambda own: uneven(own, SLOTS, TOK_DEV, LMAX, 2))(jax.random.split(key_of[3], N_DP * N_TABLE)).reshape((N_DP, N_TABLE, SLOTS)).astype(jnp.int32)
    cotangent = gaussian(key_of[4], (N_DP, TOKENS_G, D), 1.0, 6.0, ((0, 8), (1, 32)))
    w_proj = gaussian(key_of[5], (D, 4 * HEADS * HEAD_DIM), D ** -0.5, 0.25)
    w_out = gaussian(key_of[6], (HEADS * HEAD_DIM, D), (HEADS * HEAD_DIM) ** -0.5, 0.25)
    norm_gain = jnp.clip(1.0 + 0.1 * jax.random.normal(key_of[7], (D,), jnp.float32), 0.5, 1.5)
    return dict(table_rows=table_rows, item_shard=item_shard, item_slot=item_slot, seq_lengths=seq_lengths, cotangent=cotangent, w_proj=w_proj, w_out=w_out, norm_gain=norm_gain)


norm_eps = 1e-05
step_eps = 1e-06

def normalize(values):
    centered = values - lax.optimization_barrier(jnp.mean(values, axis=-1, keepdims=True))
    variance = lax.optimization_barrier(jnp.mean(centered * centered, axis=-1, keepdims=True))
    return centered * lax.rsqrt(variance + norm_eps)

def input_norm(inputs, norm_gain):
    return normalize(inputs) * norm_gain

def gate_norm(mixed_rows, gate_up):
    return normalize(mixed_rows) * gate_up

def silu_slope(values):
    sigmoid = jax.nn.sigmoid(values)
    return sigmoid * (1.0 + values * (1.0 - sigmoid))

def segment_ids(lengths, tok_count):
    seq_ends = jnp.cumsum(lengths)
    places = jnp.arange(tok_count, dtype=jnp.int32)
    return lax.optimization_barrier(jnp.sum((seq_ends[None, :] <= places[:, None]).astype(jnp.int32), axis=1))

def as_float(values):
    return values.astype(jnp.float32)

def rms_step(grads):
    return grads * lax.rsqrt(jnp.mean(grads * grads) + step_eps)

def layer_pass(fetched, lengths, upstream, w_proj, w_out, norm_gain):
    tok_count = fetched.shape[0]
    inner_width = w_out.shape[0]
    segments = segment_ids(lengths, tok_count)
    positions = jnp.arange(tok_count, dtype=jnp.int32)
    allowed = (segments[:, None] == segments[None, :]) & (positions[None, :] <= positions[:, None])
    allowed = allowed[None]
    inputs = fetched.astype(jnp.float32)
    normed = input_norm(inputs, norm_gain).astype(jnp.bfloat16)
    pre_act = jnp.dot(normed, w_proj, preferred_element_type=jnp.float32)
    activated = jax.nn.silu(pre_act).astype(jnp.bfloat16)
    gate_up = activated[:, :inner_width]
    shaped = activated[:, inner_width:].reshape(1, tok_count, 3, HEADS, HEAD_DIM)
    value_rows = shaped[:, :, 0]
    queries = shaped[:, :, 1]
    key_rows = shaped[:, :, 2]
    score_scale = HEAD_DIM ** (-0.5)
    scores = jnp.einsum('bqhd,bkhd->bhqk', as_float(queries), as_float(key_rows)) * score_scale
    weights = jnp.where(allowed[:, None], jax.nn.silu(scores), 0.0).astype(jnp.bfloat16)
    mixed_rows = jnp.einsum('bhqk,bkhd->bqhd', as_float(weights), as_float(value_rows)).reshape(tok_count, inner_width)
    gated_float, gate_back = jax.vjp(gate_norm, mixed_rows, gate_up.astype(jnp.float32))
    gated_rows = gated_float.astype(jnp.bfloat16)
    layer_rows = (inputs + jnp.dot(gated_rows, w_out, preferred_element_type=jnp.float32)).astype(jnp.bfloat16)
    grad_out_w = lax.dot_general(gated_rows, upstream, (((0,), (0,)), ((), ())), preferred_element_type=jnp.float32)
    grad_gated = lax.dot_general(upstream, w_out, (((1,), (1,)), ((), ())), preferred_element_type=jnp.float32)
    grad_mixed_float, grad_up = gate_back(grad_gated)
    grad_mixed = grad_mixed_float.astype(jnp.bfloat16).reshape(1, tok_count, HEADS, HEAD_DIM)
    grad_weights = jnp.einsum('bqhd,bkhd->bhqk', as_float(grad_mixed), as_float(value_rows))
    grad_values = jnp.einsum('bhqk,bqhd->bkhd', as_float(weights), as_float(grad_mixed))
    grad_scores = (jnp.where(allowed[:, None], grad_weights * silu_slope(scores), 0.0) * score_scale).astype(jnp.bfloat16)
    grad_queries = jnp.einsum('bhqk,bkhd->bqhd', as_float(grad_scores), as_float(key_rows))
    grad_keys = jnp.einsum('bhqk,bqhd->bkhd', as_float(grad_scores), as_float(queries))
    grad_acted = jnp.concatenate([grad_up, grad_values.reshape(tok_count, inner_width), grad_queries.reshape(tok_count, inner_width), grad_keys.reshape(tok_count, inner_width)], axis=1)
    grad_pre = (grad_acted * silu_slope(pre_act)).astype(jnp.bfloat16)
    grad_proj_w = lax.dot_general(normed, grad_pre, (((0,), (0,)), ((), ())), preferred_element_type=jnp.float32)
    grad_normed = lax.dot_general(grad_pre, w_proj, (((1,), (1,)), ((), ())), preferred_element_type=jnp.float32)
    normed_again, norm_back = jax.vjp(input_norm, inputs, norm_gain)
    grad_inputs, grad_gain = norm_back(grad_normed)
    row_grads = upstream.astype(jnp.float32) + grad_inputs
    return (layer_rows, row_grads, grad_proj_w, grad_out_w, grad_gain)

def reference(table_rows, item_shard, item_slot, seq_lengths, cotangent, w_proj, w_out, norm_gain):
    pack_count = N_DP * N_TABLE
    rows_index = (item_shard[:, :, 0] * ROWS_DEV + item_slot).reshape(pack_count, TOK_DEV).astype(jnp.int32)
    lengths = seq_lengths.reshape(pack_count, SLOTS)
    upstream = cotangent.reshape(pack_count, TOK_DEV, D)

    def one_pack(running, pack_data):
        index_rows, lengths_here, upstream_here = pack_data
        fetched = jnp.take(table_rows, index_rows, axis=0)
        layer_rows, row_grads, grad_proj_w, grad_out_w, grad_gain = layer_pass(fetched, lengths_here, upstream_here, w_proj, w_out, norm_gain)
        table_grad = running[0].at[index_rows].add(row_grads)
        return ((table_grad, running[1] + grad_proj_w, running[2] + grad_out_w, running[3] + grad_gain), layer_rows)
    initial = (jnp.zeros((VOCAB, D), jnp.float32), jnp.zeros(w_proj.shape, jnp.float32), jnp.zeros(w_out.shape, jnp.float32), jnp.zeros((D,), jnp.float32))
    totals, layer_rows = lax.scan(one_pack, initial, (rows_index, lengths, upstream))
    table_grad, grad_proj_w, grad_out_w, grad_gain = totals
    layer_out = layer_rows.reshape(N_DP, TOKENS_G, D)
    return (layer_out, table_grad, rms_step(grad_proj_w).astype(jnp.bfloat16), rms_step(grad_out_w).astype(jnp.bfloat16), rms_step(grad_gain))
```

```python
import jax
import jax.numpy as jnp
from jax import lax
from jax.experimental import pallas as pl
from jax.experimental.pallas import tpu as pltpu
from jax.sharding import PartitionSpec as P

HEADS = 4
HEAD_DIM = 128
NORM_EPS = 1e-05
STEP_EPS = 1e-06
BOTH = ("table", "dp")
F32 = jnp.float32
BF16 = jnp.bfloat16
LANES = 128
VMEM = pl.BlockSpec(memory_space=pltpu.VMEM)
SMEM = pl.BlockSpec(memory_space=pltpu.SMEM)


def call(kernel, outs, *operands, specs=None, flops=0, transcendentals=0, scratch=()):
    moved = sum(v.size * v.dtype.itemsize for v in operands)
    moved += sum(v.size * v.dtype.itemsize for v in outs)
    return pl.pallas_call(
        kernel,
        out_shape=outs,
        in_specs=specs if specs is not None else [VMEM] * len(operands),
        out_specs=[VMEM] * len(outs),
        scratch_shapes=list(scratch),
        cost_estimate=pl.CostEstimate(
            flops=flops, bytes_accessed=moved, transcendentals=transcendentals
        ),
        compiler_params=pltpu.CompilerParams(vmem_limit_bytes=40 * 1024 * 1024),
    )(*operands)


def shape(dims, dtype):
    return jax.ShapeDtypeStruct(dims, dtype)


def nn(a, b):
    return jnp.dot(a, b, preferred_element_type=F32)


def nt(a, b):
    return lax.dot_general(a, b, (((1,), (1,)), ((), ())), preferred_element_type=F32)


def tn(a, b):
    return lax.dot_general(a, b, (((0,), (0,)), ((), ())), preferred_element_type=F32)


def iota(dims, axis):
    return lax.broadcasted_iota(jnp.int32, dims, axis)


def flag(mask):
    return jnp.where(mask, 1.0, 0.0).astype(BF16)


def request_kernel(shard_ref, slot_ref, request_ref, placed_ref):
    shards, capacity = request_ref.shape
    tokens = slot_ref.shape[1]
    target = shard_ref[...]
    named = target == iota((shards, tokens), 0)
    earlier = flag(iota((tokens, tokens), 0) < iota((tokens, tokens), 1))
    counts = nn(flag(named), earlier)
    rank = jnp.sum(jnp.where(named, counts, 0.0), axis=0, keepdims=True).astype(jnp.int32)
    placed_ref[...] = target * capacity + rank
    wanted = slot_ref[...] + 1
    at_rank = rank == iota((capacity, tokens), 0)
    high = jnp.where(at_rank, wanted // 64, 0).astype(F32).astype(BF16)
    low = jnp.where(at_rank, wanted % 64, 0).astype(F32).astype(BF16)
    picked = nt(flag(named), high) * 64.0 + nt(flag(named), low)
    request_ref[...] = picked.astype(jnp.int32) - 1


def halves(values):
    shifted = values + 1
    high = (shifted // 64).astype(F32).astype(BF16)
    low = (shifted % 64).astype(F32).astype(BF16)
    return high, low


def pick_kernel(asked_ref, table_ref, out_ref):
    shards, capacity = asked_ref.shape
    slots = shards * capacity
    rows = table_ref.shape[0]
    high, low = halves(asked_ref[...])
    owner = flag(iota((slots, shards), 0) // capacity == iota((slots, shards), 1))
    spread = nn(owner, high) * 64.0 + nn(owner, low)
    mine = iota((slots, capacity), 0) % capacity == iota((slots, capacity), 1)
    wanted = jnp.sum(jnp.where(mine, spread, 0.0), axis=1, keepdims=True).astype(jnp.int32) - 1
    for start in range(0, slots, 256):
        hits = flag(wanted[start : start + 256] == iota((256, rows), 1))
        out_ref[pl.ds(start, 256), :] = nn(hits, table_ref[...]).astype(BF16)


def dense_kernel(asked_ref, got_ref, out_ref):
    shards, capacity = asked_ref.shape
    slots = shards * capacity
    rows = out_ref.shape[0]
    high, low = halves(asked_ref[...])
    column = flag(iota((capacity, slots), 0) == iota((capacity, slots), 1) % capacity)
    spread = nn(high, column) * 64.0 + nn(low, column)
    mine = iota((shards, slots), 0) == iota((shards, slots), 1) // capacity
    wanted = jnp.sum(jnp.where(mine, spread, 0.0), axis=0, keepdims=True).astype(jnp.int32) - 1
    got = got_ref[...]
    for start in range(0, rows, 256):
        hits = flag(wanted == iota((256, slots), 0) + start)
        out_ref[pl.ds(start, 256), :] = nn(hits, got).astype(BF16)


def centered_norm(values):
    centered = values - jnp.mean(values, axis=-1, keepdims=True)
    inverse = lax.rsqrt(jnp.mean(centered * centered, axis=-1, keepdims=True) + NORM_EPS)
    return centered * inverse, inverse


def norm_slope(grads, normed, inverse):
    return inverse * (
        grads
        - jnp.mean(grads, axis=-1, keepdims=True)
        - normed * jnp.mean(grads * normed, axis=-1, keepdims=True)
    )


def layer_kernel(
    lengths_ref, returned_ref, placed_ref, upstream_ref, w_proj_ref, w_out_ref, gain_ref,
    layer_ref, sent_ref, grads_ref, slope_ref, acted_ref, grad_pre_ref,
):
    slots = returned_ref.shape[0]
    tokens, width = upstream_ref.shape
    inner = w_out_ref.shape[0]
    placed = placed_ref[...]
    eye = iota((tokens, tokens), 0) == iota((tokens, tokens), 1)
    placed_col = jnp.sum(jnp.where(eye, placed, 0), axis=1, keepdims=True)
    inputs = nn(flag(placed_col == iota((tokens, slots), 1)), returned_ref[...])
    gain = gain_ref[...]
    hat, inverse = centered_norm(inputs)
    normed = (hat * gain).astype(BF16)
    for block in range(4):
        cols = pl.ds(block * inner, inner)
        pre = nn(normed, w_proj_ref[:, cols])
        sig = jax.nn.sigmoid(pre)
        acted_ref[:, cols] = (pre * sig).astype(BF16)
        slope_ref[:, cols] = sig * (1.0 + pre * (1.0 - sig))
    query_pos = iota((tokens, tokens), 0)
    key_pos = iota((tokens, tokens), 1)
    start_of = jnp.zeros((tokens, 1), jnp.int32)
    query_col = iota((tokens, 1), 0)
    end = jnp.int32(0)
    for i in range(lengths_ref.shape[1]):
        end = end + lengths_ref[0, i]
        start_of = jnp.where(query_col >= end, end, start_of)
    allowed = (key_pos <= query_pos) & (key_pos >= start_of)
    scale = HEAD_DIM ** (-0.5)

    def head(block, h):
        return acted_ref[:, pl.ds(block * inner + h * HEAD_DIM, HEAD_DIM)]

    mixed, weights, slopes = [], [], []
    for h in range(HEADS):
        scores = nt(head(2, h), head(3, h)) * scale
        sig = jax.nn.sigmoid(scores)
        weight = jnp.where(allowed, scores * sig, 0.0).astype(BF16)
        slopes.append(jnp.where(allowed, sig * (1.0 + scores * (1.0 - sig)), 0.0))
        weights.append(weight)
        mixed.append(nn(weight, head(1, h)))
    mixed_hat, mixed_inverse = centered_norm(jnp.concatenate(mixed, axis=1))
    gate = acted_ref[:, pl.ds(0, inner)].astype(F32)
    gated = (mixed_hat * gate).astype(BF16)
    layer_ref[...] = (inputs + nn(gated, w_out_ref[...])).astype(BF16)
    upstream = upstream_ref[...]
    grad_gated = nt(upstream, w_out_ref[...])
    grad_mixed = norm_slope(grad_gated * gate, mixed_hat, mixed_inverse).astype(BF16)

    def put(block, h, value):
        cols = pl.ds(block * inner + h * HEAD_DIM, HEAD_DIM)
        grad_pre_ref[:, cols] = (value * slope_ref[:, cols]).astype(BF16)

    grad_pre_ref[:, pl.ds(0, inner)] = (
        grad_gated * mixed_hat * slope_ref[:, pl.ds(0, inner)]
    ).astype(BF16)
    for h in range(HEADS):
        part = grad_mixed[:, h * HEAD_DIM : (h + 1) * HEAD_DIM]
        grad_scores = (nt(part, head(1, h)) * slopes[h] * scale).astype(BF16)
        put(1, h, tn(weights[h], part))
        put(2, h, nn(grad_scores, head(3, h)))
        put(3, h, tn(grad_scores, head(2, h)))
    grad_normed = nt(grad_pre_ref[...], w_proj_ref[...])
    grad_gain = jnp.sum(grad_normed * hat, axis=0, keepdims=True)
    row_grads = (
        upstream.astype(F32) + norm_slope(grad_normed * gain, hat, inverse)
    ).astype(BF16)
    sent_ref[...] = nn(flag(placed == iota((slots, tokens), 0)), row_grads).astype(BF16)

    half = grads_ref.shape[1] - 16
    per_half = half // width
    normed_t = normed.T
    gated_t = gated.T
    blocks = (4 * inner + width) // LANES
    for pair in range(0, blocks, 2):
        start = pair * LANES
        if start < 4 * inner:
            value = nn(normed_t, grad_pre_ref[:, pl.ds(start, 2 * LANES)])
        else:
            value = nn(gated_t, upstream_ref[:, pl.ds(start - 4 * inner, 2 * LANES)])
        for k in range(2):
            side, place = divmod(pair + k, per_half)
            grads_ref[side, pl.ds(place * width, width), :] = value[
                :, k * LANES : (k + 1) * LANES
            ].astype(BF16)
    tail = gain_tail(
        jnp.concatenate(
            [grad_gain[:, k * LANES : (k + 1) * LANES] for k in range(width // LANES)], axis=0
        )
    )
    for side in range(2):
        grads_ref[side, pl.ds(half, 16), :] = tail


def gain_tail(grad_gain):
    high = grad_gain.astype(BF16).astype(F32)
    low = grad_gain - high
    return jnp.concatenate([high, low, jnp.zeros((8, LANES), F32)], axis=0).astype(BF16)


def merge_kernel(in_ref, out_ref):
    parts = in_ref.shape[0]
    rows = in_ref.shape[1] - 16
    pieces, size, _ = out_ref.shape
    chunk = rows // pieces

    def total(start, count):
        value = in_ref[0, pl.ds(start, count), :].astype(F32)
        for i in range(1, parts):
            value = value + in_ref[i, pl.ds(start, count), :].astype(F32)
        return value

    tail = total(rows, 16)
    tail = gain_tail(tail[0:4] + tail[4:8]).astype(F32)
    whole = size == chunk + 16
    for p in range(pieces):
        if whole:
            out_ref[p, pl.ds(0, chunk), :] = total(p * chunk, chunk).astype(BF16)
            out_ref[p, pl.ds(chunk, 16), :] = tail.astype(BF16)
        elif p % 2 == 0:
            two = total(p * chunk, 2 * chunk)
            for k in range(2):
                piece = jnp.concatenate([two[k * chunk : (k + 1) * chunk], tail[0:8]], axis=0)
                out_ref[p + k] = piece.astype(BF16)


def turn_kernel(in_ref, spread_ref, gain_ref):
    total = jnp.sum(in_ref[...].astype(F32), axis=0)
    rows = spread_ref.shape[1]
    mine = total[0:rows].astype(BF16)
    for p in range(spread_ref.shape[0]):
        spread_ref[p] = mine
    gain = total[rows : rows + 4] + total[rows + 4 : rows + 8]
    scale = lax.rsqrt(jnp.sum(gain * gain) / gain.size + STEP_EPS)
    gain_ref[...] = gain * scale


def finish_kernel(grads_ref, proj_ref, out_ref):
    rows = proj_ref.shape[0]
    proj_blocks = proj_ref.shape[1] // LANES
    out_blocks = out_ref.shape[1] // LANES

    def squares(first, count):
        total = jnp.zeros((8, LANES), F32)
        for b in range(first, first + count):
            value = grads_ref[pl.ds(b * rows, rows), :].astype(F32)
            total = total + jnp.sum((value * value).reshape(rows // 8, 8, LANES), axis=0)
        return jnp.sum(total)

    proj_scale = lax.rsqrt(squares(0, proj_blocks) / proj_ref.size + STEP_EPS)
    out_scale = lax.rsqrt(squares(proj_blocks, out_blocks) / out_ref.size + STEP_EPS)
    for b in range(proj_blocks + out_blocks):
        value = grads_ref[pl.ds(b * rows, rows), :].astype(F32)
        if b < proj_blocks:
            proj_ref[:, pl.ds(b * LANES, LANES)] = (value * proj_scale).astype(BF16)
        else:
            cols = pl.ds((b - proj_blocks) * LANES, LANES)
            out_ref[:, cols] = (value * out_scale).astype(BF16)


ZS, XS, YS = 8, 4, 4


def device(z, x, y, c):
    return (z * XS + x) * (2 * YS) + y * 2 + c


CORE_GROUPS = [
    [device(z, x, y, c) for c in range(2)] for z in range(ZS) for x in range(XS) for y in range(YS)
]
FIRST_GROUPS = [
    [device(z, x, y, 0) for x in range(XS)] for z in range(ZS) for y in range(YS)
] + [[device(z, x, y, 1) for y in range(YS)] for z in range(ZS) for x in range(XS)]
SECOND_GROUPS = [
    [device(z, x, y, 0) for y in range(YS)] for z in range(ZS) for x in range(XS)
] + [[device(z, x, y, 1) for x in range(XS)] for z in range(ZS) for y in range(YS)]
LAST_GROUPS = [
    [device(z, x, y, c) for z in range(ZS)]
    for x in range(XS)
    for y in range(YS)
    for c in range(2)
]


def swap(values, groups):
    return lax.all_to_all(
        values, BOTH, split_axis=0, concat_axis=0, tiled=True, axis_index_groups=groups
    )


def spread(values, groups):
    count = len(groups[0])
    return swap(jnp.broadcast_to(values[None], (count, *values.shape)), groups).reshape(
        count * values.shape[0], values.shape[1]
    )


def body(table_rows, item_shard, item_slot, seq_lengths, cotangent, w_proj, w_out, norm_gain):
    shards = lax.axis_size("table")
    tokens = item_slot.shape[1]
    width = table_rows.shape[1]
    inner = w_out.shape[0]
    capacity = 2 * tokens // shards
    slots = shards * capacity
    requests, placed = call(
        request_kernel,
        [shape((shards, capacity), jnp.int32), shape((1, tokens), jnp.int32)],
        item_shard.reshape(1, tokens),
        item_slot,
    )
    asked = lax.all_to_all(requests, "table", split_axis=0, concat_axis=0, tiled=True)
    (picked,) = call(
        pick_kernel,
        [shape((slots, width), BF16)],
        asked,
        table_rows,
        flops=2 * slots * width * table_rows.shape[0],
    )
    returned = lax.all_to_all(
        picked.reshape(shards, capacity, width), "table", split_axis=0, concat_axis=0, tiled=True
    ).reshape(slots, width)
    half = width * (4 * inner + width) // (2 * LANES)
    layer_rows, sent, grads = call(
        layer_kernel,
        [
            shape((tokens, width), BF16),
            shape((slots, width), BF16),
            shape((2, half + 16, LANES), BF16),
        ],
        seq_lengths[0],
        returned,
        placed,
        cotangent[0],
        w_proj,
        w_out,
        norm_gain.reshape(1, width),
        specs=[SMEM] + [VMEM] * 6,
        flops=6 * tokens * width * (4 * inner + width),
        transcendentals=tokens * (4 * inner + HEADS * tokens),
        scratch=[
            pltpu.VMEM((tokens, 4 * inner), F32),
            pltpu.VMEM((tokens, 4 * inner), BF16),
            pltpu.VMEM((tokens, 4 * inner), BF16),
        ],
    )
    got = lax.all_to_all(
        sent.reshape(shards, capacity, width), "table", split_axis=0, concat_axis=0, tiled=True
    ).reshape(slots, width)
    (dense,) = call(
        dense_kernel,
        [shape(table_rows.shape, BF16)],
        asked,
        got,
        flops=2 * slots * width * table_rows.shape[0],
    )
    table_grad = lax.psum_scatter(dense, "dp", scatter_dimension=0, tiled=True).astype(F32)

    grads = swap(grads, CORE_GROUPS)
    (grads,) = call(merge_kernel, [shape((4, half // 4 + 16, LANES), BF16)], grads)
    grads = swap(grads, FIRST_GROUPS)
    (grads,) = call(merge_kernel, [shape((4, half // 16 + 16, LANES), BF16)], grads)
    grads = swap(grads, SECOND_GROUPS)
    (grads,) = call(merge_kernel, [shape((8, half // 128 + 8, LANES), BF16)], grads)
    grads = swap(grads, LAST_GROUPS)
    grads, step_gain = call(
        turn_kernel,
        [shape((8, half // 128, LANES), BF16), shape((width // LANES, LANES), F32)],
        grads,
    )
    grads = swap(grads, LAST_GROUPS).reshape(half // 16, LANES)
    grads = spread(grads, SECOND_GROUPS)
    grads = spread(grads, FIRST_GROUPS)
    grads = spread(grads, CORE_GROUPS)
    step_proj, step_out = call(
        finish_kernel, [shape(w_proj.shape, BF16), shape(w_out.shape, BF16)], grads
    )
    return (layer_rows[None], table_grad, step_proj, step_out, step_gain.reshape(width))


def solution(mesh):
    placed = (
        P("table", None),
        P("dp", "table", None),
        P("dp", "table"),
        P("dp", "table", None),
        P("dp", "table", None),
        P(),
        P(),
        P(),
    )
    return jax.shard_map(
        body,
        mesh=mesh,
        in_specs=placed,
        out_specs=(P("dp", "table", None), P(("table", "dp"), None), P(), P(), P()),
        check_vma=False,
    )
```

```python
import jax
import jax.numpy as jnp
from jax import lax
from jax.experimental import pallas as pl
from jax.experimental.pallas import tpu as pltpu
from jax.sharding import PartitionSpec as P

HEADS = 4
HEAD_DIM = 128
NORM_EPS = 1e-05
STEP_EPS = 1e-06
BOTH = ("table", "dp")
F32 = jnp.float32
BF16 = jnp.bfloat16
LANES = 128
VMEM = pl.BlockSpec(memory_space=pltpu.VMEM)
SMEM = pl.BlockSpec(memory_space=pltpu.SMEM)


def call(kernel, outs, *operands, specs=None, flops=0, transcendentals=0, scratch=()):
    moved = sum(v.size * v.dtype.itemsize for v in operands)
    moved += sum(v.size * v.dtype.itemsize for v in outs)
    return pl.pallas_call(
        kernel,
        out_shape=outs,
        in_specs=specs if specs is not None else [VMEM] * len(operands),
        out_specs=[VMEM] * len(outs),
        scratch_shapes=list(scratch),
        cost_estimate=pl.CostEstimate(
            flops=flops, bytes_accessed=moved, transcendentals=transcendentals
        ),
        compiler_params=pltpu.CompilerParams(vmem_limit_bytes=40 * 1024 * 1024),
    )(*operands)


def shape(dims, dtype):
    return jax.ShapeDtypeStruct(dims, dtype)


def nn(a, b):
    return jnp.dot(a, b, preferred_element_type=F32)


def nt(a, b):
    return lax.dot_general(a, b, (((1,), (1,)), ((), ())), preferred_element_type=F32)


def tn(a, b):
    return lax.dot_general(a, b, (((0,), (0,)), ((), ())), preferred_element_type=F32)


def iota(dims, axis):
    return lax.broadcasted_iota(jnp.int32, dims, axis)


def flag(mask):
    return jnp.where(mask, 1.0, 0.0).astype(BF16)


def request_kernel(shard_ref, slot_ref, request_ref, placed_ref):
    shards, capacity = request_ref.shape
    tokens = slot_ref.shape[1]
    target = shard_ref[...]
    named = target == iota((shards, tokens), 0)
    earlier = flag(iota((tokens, tokens), 0) < iota((tokens, tokens), 1))
    counts = nn(flag(named), earlier)
    rank = jnp.sum(jnp.where(named, counts, 0.0), axis=0, keepdims=True).astype(jnp.int32)
    placed_ref[...] = target * capacity + rank
    wanted = slot_ref[...] + 1
    at_rank = rank == iota((capacity, tokens), 0)
    high = jnp.where(at_rank, wanted // 64, 0).astype(F32).astype(BF16)
    low = jnp.where(at_rank, wanted % 64, 0).astype(F32).astype(BF16)
    picked = nt(flag(named), high) * 64.0 + nt(flag(named), low)
    request_ref[...] = picked.astype(jnp.int32) - 1


def halves(values):
    shifted = values + 1
    high = (shifted // 64).astype(F32).astype(BF16)
    low = (shifted % 64).astype(F32).astype(BF16)
    return high, low


def pick_kernel(asked_ref, table_ref, out_ref):
    shards, capacity = asked_ref.shape
    slots = shards * capacity
    rows = table_ref.shape[0]
    high, low = halves(asked_ref[...])
    owner = flag(iota((slots, shards), 0) // capacity == iota((slots, shards), 1))
    spread = nn(owner, high) * 64.0 + nn(owner, low)
    mine = iota((slots, capacity), 0) % capacity == iota((slots, capacity), 1)
    wanted = jnp.sum(jnp.where(mine, spread, 0.0), axis=1, keepdims=True).astype(jnp.int32) - 1
    for start in range(0, slots, 256):
        hits = flag(wanted[start : start + 256] == iota((256, rows), 1))
        out_ref[pl.ds(start, 256), :] = nn(hits, table_ref[...]).astype(BF16)


def dense_kernel(asked_ref, got_ref, keep_ref, give_ref):
    shards, capacity = asked_ref.shape
    slots = shards * capacity
    ring, rows, _ = keep_ref.shape
    high, low = halves(asked_ref[...])
    column = flag(iota((capacity, slots), 0) == iota((capacity, slots), 1) % capacity)
    spread = nn(high, column) * 64.0 + nn(low, column)
    mine = iota((shards, slots), 0) == iota((shards, slots), 1) // capacity
    wanted = jnp.sum(jnp.where(mine, spread, 0.0), axis=0, keepdims=True).astype(jnp.int32) - 1
    got = got_ref[...]
    rank = lax.axis_index("dp")
    core, place = lax.rem(rank, 2), lax.div(rank, 2)
    for out_ref, side in ((give_ref, 1 - core), (keep_ref, core)):
        for d in range(ring):
            first = (lax.rem(place + d, ring) * 2 + side) * rows
            hits = flag(wanted - first == iota((rows, slots), 0))
            out_ref[d] = nn(hits, got).astype(BF16)


def pair_kernel(mine_ref, other_ref, *out_refs):
    for d, out_ref in enumerate(out_refs):
        out_ref[...] = (mine_ref[d].astype(F32) + other_ref[d].astype(F32)).astype(BF16)


def centered_norm(values):
    centered = values - jnp.mean(values, axis=-1, keepdims=True)
    inverse = lax.rsqrt(jnp.mean(centered * centered, axis=-1, keepdims=True) + NORM_EPS)
    return centered * inverse, inverse


def norm_slope(grads, normed, inverse):
    return inverse * (
        grads
        - jnp.mean(grads, axis=-1, keepdims=True)
        - normed * jnp.mean(grads * normed, axis=-1, keepdims=True)
    )


def layer_kernel(
    lengths_ref, returned_ref, placed_ref, upstream_ref, w_proj_ref, w_out_ref, gain_ref,
    layer_ref, sent_ref, keep_ref, give_ref, slope_ref, acted_ref, grad_pre_ref,
):
    slots = returned_ref.shape[0]
    tokens, width = upstream_ref.shape
    inner = w_out_ref.shape[0]
    placed = placed_ref[...]
    eye = iota((tokens, tokens), 0) == iota((tokens, tokens), 1)
    placed_col = jnp.sum(jnp.where(eye, placed, 0), axis=1, keepdims=True)
    inputs = nn(flag(placed_col == iota((tokens, slots), 1)), returned_ref[...])
    gain = gain_ref[...]
    hat, inverse = centered_norm(inputs)
    normed = (hat * gain).astype(BF16)
    for block in range(4):
        cols = pl.ds(block * inner, inner)
        pre = nn(normed, w_proj_ref[:, cols])
        sig = jax.nn.sigmoid(pre)
        acted_ref[:, cols] = (pre * sig).astype(BF16)
        slope_ref[:, cols] = sig * (1.0 + pre * (1.0 - sig))
    query_pos = iota((tokens, tokens), 0)
    key_pos = iota((tokens, tokens), 1)
    start_of = jnp.zeros((tokens, 1), jnp.int32)
    query_col = iota((tokens, 1), 0)
    end = jnp.int32(0)
    for i in range(lengths_ref.shape[1]):
        end = end + lengths_ref[0, i]
        start_of = jnp.where(query_col >= end, end, start_of)
    allowed = (key_pos <= query_pos) & (key_pos >= start_of)
    scale = HEAD_DIM ** (-0.5)

    def head(block, h):
        return acted_ref[:, pl.ds(block * inner + h * HEAD_DIM, HEAD_DIM)]

    mixed, weights, slopes = [], [], []
    for h in range(HEADS):
        scores = nt(head(2, h), head(3, h)) * scale
        sig = jax.nn.sigmoid(scores)
        weight = jnp.where(allowed, scores * sig, 0.0).astype(BF16)
        slopes.append(jnp.where(allowed, sig * (1.0 + scores * (1.0 - sig)), 0.0))
        weights.append(weight)
        mixed.append(nn(weight, head(1, h)))
    mixed_hat, mixed_inverse = centered_norm(jnp.concatenate(mixed, axis=1))
    gate = acted_ref[:, pl.ds(0, inner)].astype(F32)
    gated = (mixed_hat * gate).astype(BF16)
    layer_ref[...] = (inputs + nn(gated, w_out_ref[...])).astype(BF16)
    upstream = upstream_ref[...]
    grad_gated = nt(upstream, w_out_ref[...])
    grad_mixed = norm_slope(grad_gated * gate, mixed_hat, mixed_inverse).astype(BF16)

    def put(block, h, value):
        cols = pl.ds(block * inner + h * HEAD_DIM, HEAD_DIM)
        grad_pre_ref[:, cols] = (value * slope_ref[:, cols]).astype(BF16)

    grad_pre_ref[:, pl.ds(0, inner)] = (
        grad_gated * mixed_hat * slope_ref[:, pl.ds(0, inner)]
    ).astype(BF16)
    for h in range(HEADS):
        part = grad_mixed[:, h * HEAD_DIM : (h + 1) * HEAD_DIM]
        grad_scores = (nt(part, head(1, h)) * slopes[h] * scale).astype(BF16)
        put(1, h, tn(weights[h], part))
        put(2, h, nn(grad_scores, head(3, h)))
        put(3, h, tn(grad_scores, head(2, h)))
    grad_normed = nt(grad_pre_ref[...], w_proj_ref[...])
    grad_gain = jnp.sum(grad_normed * hat, axis=0, keepdims=True)
    row_grads = (
        upstream.astype(F32) + norm_slope(grad_normed * gain, hat, inverse)
    ).astype(BF16)
    sent_ref[...] = nn(flag(placed == iota((slots, tokens), 0)), row_grads).astype(BF16)

    half = keep_ref.shape[0] - 16
    per_half = half // width
    core = lax.rem(lax.axis_index("dp"), 2)
    normed_t = normed.T
    gated_t = gated.T
    blocks = (4 * inner + width) // LANES

    def store(side, rows, value):
        @pl.when(core == side)
        def _():
            keep_ref[rows, :] = value

        @pl.when(core != side)
        def _():
            give_ref[rows, :] = value

    for pair in range(0, blocks, 2):
        start = pair * LANES
        if start < 4 * inner:
            value = nn(normed_t, grad_pre_ref[:, pl.ds(start, 2 * LANES)])
        else:
            value = nn(gated_t, upstream_ref[:, pl.ds(start - 4 * inner, 2 * LANES)])
        for k in range(2):
            side, place = divmod(pair + k, per_half)
            part = value[:, k * LANES : (k + 1) * LANES].astype(BF16)
            store(side, pl.ds(place * width, width), part)
    tail = gain_tail(
        jnp.concatenate(
            [grad_gain[:, k * LANES : (k + 1) * LANES] for k in range(width // LANES)], axis=0
        )
    )
    keep_ref[pl.ds(half, 16), :] = tail
    give_ref[pl.ds(half, 16), :] = tail


def gain_tail(grad_gain):
    high = grad_gain.astype(BF16).astype(F32)
    low = grad_gain - high
    return jnp.concatenate([high, low, jnp.zeros((8, LANES), F32)], axis=0).astype(BF16)


def first_place():
    rank = lax.axis_index("dp")
    along_x = lax.rem(lax.axis_index("table"), XS)
    along_y = lax.div(rank, 2)
    core = lax.rem(rank, 2)
    return core, jnp.where(core == 0, along_x, along_y), jnp.where(core == 0, along_y, along_x)


def part_sum(refs, start, count):
    value = refs[0][pl.ds(start, count), :].astype(F32)
    for ref in refs[1:]:
        value = value + ref[pl.ds(start, count), :].astype(F32)
    return value


def tail_sum(refs, rows):
    tail = part_sum(refs, rows, 16)
    return gain_tail(tail[0:4] + tail[4:8])


def turned_merge_kernel(mine_ref, other_ref, *out_refs):
    refs = (mine_ref, other_ref)
    chunk = out_refs[0].shape[0] - 16
    ring = len(out_refs)
    tail = tail_sum(refs, ring * chunk)
    _, place, _ = first_place()
    for d in (1, 2, 3, 0):
        start = pl.multiple_of(lax.rem(place + d, ring) * chunk, chunk)
        out_refs[d][pl.ds(0, chunk), :] = part_sum(refs, start, chunk).astype(BF16)
        out_refs[d][pl.ds(chunk, 16), :] = tail


def merge_kernel(*refs):
    refs, out_ref = refs[:-1], refs[-1]
    pieces, size, _ = out_ref.shape
    chunk = size - 16
    tail = tail_sum(refs, pieces * chunk)
    for p in range(pieces):
        out_ref[p, pl.ds(0, chunk), :] = part_sum(refs, p * chunk, chunk).astype(BF16)
        out_ref[p, pl.ds(chunk, 16), :] = tail


def narrow_merge_kernel(in_ref, out_ref):
    pieces, size, _ = out_ref.shape
    chunk = size - 8
    refs = [in_ref.at[i] for i in range(in_ref.shape[0])]
    tail = tail_sum(refs, pieces * chunk).astype(F32)[0:8]
    for p in range(0, pieces, 2):
        two = part_sum(refs, p * chunk, 2 * chunk)
        for k in range(2):
            piece = jnp.concatenate([two[k * chunk : (k + 1) * chunk], tail], axis=0)
            out_ref[p + k] = piece.astype(BF16)


def turn_kernel(in_ref, spread_ref, gain_ref):
    total = jnp.sum(in_ref[...].astype(F32), axis=0)
    rows = spread_ref.shape[1]
    mine = total[0:rows].astype(BF16)
    for p in range(spread_ref.shape[0]):
        spread_ref[p] = mine
    gain = total[rows : rows + 4] + total[rows + 4 : rows + 8]
    scale = lax.rsqrt(jnp.sum(gain * gain) / gain.size + STEP_EPS)
    gain_ref[...] = gain * scale


def finish_kernel(*refs):
    pieces, (proj_ref, out_ref, grads_ref, sems) = refs[:-4], refs[-4:]
    rows = proj_ref.shape[0]
    proj_blocks = proj_ref.shape[1] // LANES
    out_blocks = out_ref.shape[1] // LANES
    ring = len(pieces) // 2
    chunk = pieces[0].shape[0]
    core, mine, other = first_place()
    copies = []
    for i, piece in enumerate(pieces):
        side, place = (core, mine) if i < ring else (1 - core, other)
        spot = side * ring + lax.rem(place + (ring - i % ring), ring)
        start = pl.multiple_of(spot * chunk, chunk)
        copies.append(
            pltpu.make_async_copy(piece, grads_ref.at[pl.ds(start, chunk), :], sems.at[i])
        )
    for copy in copies:
        copy.start()
    for copy in copies:
        copy.wait()

    def squares(first, count):
        total = jnp.zeros((8, LANES), F32)
        for b in range(first, first + count):
            value = grads_ref[pl.ds(b * rows, rows), :].astype(F32)
            total = total + jnp.sum((value * value).reshape(rows // 8, 8, LANES), axis=0)
        return jnp.sum(total)

    proj_scale = lax.rsqrt(squares(0, proj_blocks) / proj_ref.size + STEP_EPS)
    out_scale = lax.rsqrt(squares(proj_blocks, out_blocks) / out_ref.size + STEP_EPS)
    for b in range(proj_blocks + out_blocks):
        value = grads_ref[pl.ds(b * rows, rows), :].astype(F32)
        if b < proj_blocks:
            proj_ref[:, pl.ds(b * LANES, LANES)] = (value * proj_scale).astype(BF16)
        else:
            cols = pl.ds((b - proj_blocks) * LANES, LANES)
            out_ref[:, cols] = (value * out_scale).astype(BF16)


def sum_kernel(*refs):
    value = refs[0][...].astype(F32)
    for ref in refs[1:-1]:
        value = value + ref[...].astype(F32)
    refs[-1][...] = value


ZS, XS, YS = 8, 4, 4


def device(z, x, y, c):
    return (z * XS + x) * (2 * YS) + y * 2 + c


PLACES = [(z, x, y, c) for z in range(ZS) for x in range(XS) for y in range(YS) for c in range(2)]
CORE_PERM = [(device(z, x, y, c), device(z, x, y, 1 - c)) for z, x, y, c in PLACES]


def first_perm(d):
    return [
        (
            device(z, x, y, c),
            device(z, (x + d) % XS, y, c) if c == 0 else device(z, x, (y + d) % YS, c),
        )
        for z, x, y, c in PLACES
    ]


def y_perm(d):
    return [(device(z, x, y, c), device(z, x, (y + d) % YS, c)) for z, x, y, c in PLACES]


SECOND_GROUPS = [
    [device(z, x, y, 0) for y in range(YS)] for z in range(ZS) for x in range(XS)
] + [[device(z, x, y, 1) for x in range(XS)] for z in range(ZS) for y in range(YS)]
LAST_GROUPS = [
    [device(z, x, y, c) for z in range(ZS)]
    for x in range(XS)
    for y in range(YS)
    for c in range(2)
]


def swap(values, groups):
    return lax.all_to_all(
        values, BOTH, split_axis=0, concat_axis=0, tiled=True, axis_index_groups=groups
    )


def spread(values, groups):
    count = len(groups[0])
    return swap(jnp.broadcast_to(values[None], (count, *values.shape)), groups).reshape(
        count * values.shape[0], values.shape[1]
    )


def body(table_rows, item_shard, item_slot, seq_lengths, cotangent, w_proj, w_out, norm_gain):
    shards = lax.axis_size("table")
    tokens = item_slot.shape[1]
    width = table_rows.shape[1]
    inner = w_out.shape[0]
    capacity = 2 * tokens // shards
    slots = shards * capacity
    requests, placed = call(
        request_kernel,
        [shape((shards, capacity), jnp.int32), shape((1, tokens), jnp.int32)],
        item_shard.reshape(1, tokens),
        item_slot,
    )
    asked = lax.all_to_all(requests, "table", split_axis=0, concat_axis=0, tiled=True)
    (picked,) = call(
        pick_kernel,
        [shape((slots, width), BF16)],
        asked,
        table_rows,
        flops=2 * slots * width * table_rows.shape[0],
    )
    returned = lax.all_to_all(
        picked.reshape(shards, capacity, width), "table", split_axis=0, concat_axis=0, tiled=True
    ).reshape(slots, width)
    half = width * (4 * inner + width) // (2 * LANES)
    grad_half = shape((half + 16, LANES), BF16)
    layer_rows, sent, keep, give = call(
        layer_kernel,
        [
            shape((tokens, width), BF16),
            shape((slots, width), BF16),
            grad_half,
            grad_half,
        ],
        seq_lengths[0],
        returned,
        placed,
        cotangent[0],
        w_proj,
        w_out,
        norm_gain.reshape(1, width),
        specs=[SMEM] + [VMEM] * 6,
        flops=6 * tokens * width * (4 * inner + width),
        transcendentals=tokens * (4 * inner + HEADS * tokens),
        scratch=[
            pltpu.VMEM((tokens, 4 * inner), F32),
            pltpu.VMEM((tokens, 4 * inner), BF16),
            pltpu.VMEM((tokens, 4 * inner), BF16),
        ],
    )
    got = lax.all_to_all(
        sent.reshape(shards, capacity, width), "table", split_axis=0, concat_axis=0, tiled=True
    ).reshape(slots, width)
    rows = table_rows.shape[0] // (2 * YS)
    quarter = shape((YS, rows, width), BF16)
    kept, given = call(
        dense_kernel,
        [quarter, quarter],
        asked,
        got,
        flops=2 * slots * width * table_rows.shape[0],
    )
    given = lax.ppermute(given, BOTH, CORE_PERM)
    parts = call(pair_kernel, [shape((rows, width), BF16)] * YS, kept, given)
    parts = [parts[0]] + [lax.ppermute(parts[d], BOTH, y_perm(d)) for d in (1, 2, 3)]
    (table_grad,) = call(sum_kernel, [shape((rows, width), F32)], *parts)

    other = lax.ppermute(give, BOTH, CORE_PERM)
    parts = call(turned_merge_kernel, [shape((half // 4 + 16, LANES), BF16)] * 4, keep, other)
    parts = [parts[0]] + [lax.ppermute(parts[d], BOTH, first_perm(d)) for d in (1, 2, 3)]
    (grads,) = call(merge_kernel, [shape((4, half // 16 + 16, LANES), BF16)], *parts)
    grads = swap(grads, SECOND_GROUPS)
    (grads,) = call(narrow_merge_kernel, [shape((8, half // 128 + 8, LANES), BF16)], grads)
    grads = swap(grads, LAST_GROUPS)
    grads, step_gain = call(
        turn_kernel,
        [shape((8, half // 128, LANES), BF16), shape((width // LANES, LANES), F32)],
        grads,
    )
    grads = swap(grads, LAST_GROUPS).reshape(half // 16, LANES)
    grads = spread(grads, SECOND_GROUPS)
    mine = [grads] + [lax.ppermute(grads, BOTH, first_perm(d)) for d in (1, 2, 3)]
    others = [lax.ppermute(piece, BOTH, CORE_PERM) for piece in mine]
    step_proj, step_out = call(
        finish_kernel,
        [shape(w_proj.shape, BF16), shape(w_out.shape, BF16)],
        *mine,
        *others,
        specs=[pl.BlockSpec(memory_space=pl.ANY)] * 8,
        scratch=[pltpu.VMEM((2 * half, LANES), BF16), pltpu.SemaphoreType.DMA((8,))],
    )
    return (layer_rows[None], table_grad, step_proj, step_out, step_gain.reshape(width))


def solution(mesh):
    placed = (
        P("table", None),
        P("dp", "table", None),
        P("dp", "table"),
        P("dp", "table", None),
        P("dp", "table", None),
        P(),
        P(),
        P(),
    )
    return jax.shard_map(
        body,
        mesh=mesh,
        in_specs=placed,
        out_specs=(P("dp", "table", None), P(("table", "dp"), None), P(), P(), P()),
        check_vma=False,
    )
```

```python
import functools

import jax
import jax.numpy as jnp
from jax import lax
from jax.experimental import pallas as pl
from jax.experimental.pallas import tpu as pltpu
from jax.sharding import PartitionSpec as P

HEADS = 4
HEAD_DIM = 128
NORM_EPS = 1e-05
STEP_EPS = 1e-06
BOTH = ("table", "dp")
F32 = jnp.float32
BF16 = jnp.bfloat16
LANES = 128
STRIP = 64
VMEM = pl.BlockSpec(memory_space=pltpu.VMEM)
SMEM = pl.BlockSpec(memory_space=pltpu.SMEM)
ANY = pl.BlockSpec(memory_space=pl.ANY)
HBM = pl.BlockSpec(memory_space=pltpu.HBM)


def call(
    kernel, outs, *operands, specs=None, out_specs=None, flops=0, transcendentals=0, scratch=(),
    aliases=None,
):
    moved = sum(v.size * v.dtype.itemsize for v in operands)
    moved += sum(v.size * v.dtype.itemsize for v in outs)
    return pl.pallas_call(
        kernel,
        out_shape=outs,
        in_specs=specs if specs is not None else [VMEM] * len(operands),
        out_specs=out_specs if out_specs is not None else [VMEM] * len(outs),
        scratch_shapes=list(scratch),
        input_output_aliases=aliases or {},
        cost_estimate=pl.CostEstimate(
            flops=flops, bytes_accessed=moved, transcendentals=transcendentals
        ),
        compiler_params=pltpu.CompilerParams(vmem_limit_bytes=40 * 1024 * 1024),
    )(*operands)


def shape(dims, dtype):
    return jax.ShapeDtypeStruct(dims, dtype)


def nn(a, b):
    return jnp.dot(a, b, preferred_element_type=F32)


def nt(a, b):
    return lax.dot_general(a, b, (((1,), (1,)), ((), ())), preferred_element_type=F32)


def tn(a, b):
    return lax.dot_general(a, b, (((0,), (0,)), ((), ())), preferred_element_type=F32)


def iota(dims, axis):
    return lax.broadcasted_iota(jnp.int32, dims, axis)


def flag(mask):
    return jnp.where(mask, 1.0, 0.0).astype(BF16)


def request_kernel(rows, item_ref, request_ref, placed_ref):
    shards, capacity = request_ref.shape
    tokens = item_ref.shape[1]
    item = item_ref[...]
    target = item // rows
    named = target == iota((shards, tokens), 0)
    earlier = flag(iota((tokens, tokens), 0) < iota((tokens, tokens), 1))
    counts = nn(flag(named), earlier)
    rank = jnp.sum(jnp.where(named, counts, 0.0), axis=0, keepdims=True).astype(jnp.int32)
    placed_ref[...] = target * capacity + rank
    wanted = item - target * rows + 1
    at_rank = rank == iota((capacity, tokens), 0)
    high = jnp.where(at_rank, wanted // 64, 0).astype(F32).astype(BF16)
    low = jnp.where(at_rank, wanted % 64, 0).astype(F32).astype(BF16)
    picked = nt(flag(named), high) * 64.0 + nt(flag(named), low)
    request_ref[...] = picked.astype(jnp.int32) - 1


def halves(values):
    shifted = values + 1
    high = (shifted // 64).astype(F32).astype(BF16)
    low = (shifted % 64).astype(F32).astype(BF16)
    return high, low


def pick_kernel(asked_ref, table_ref, out_ref):
    shards, capacity = asked_ref.shape
    slots = shards * capacity
    rows = table_ref.shape[0]
    high, low = halves(asked_ref[...])
    owner = flag(iota((slots, shards), 0) // capacity == iota((slots, shards), 1))
    spread = nn(owner, high) * 64.0 + nn(owner, low)
    mine = iota((slots, capacity), 0) % capacity == iota((slots, capacity), 1)
    wanted = jnp.sum(jnp.where(mine, spread, 0.0), axis=1, keepdims=True).astype(jnp.int32) - 1
    for start in range(0, slots, 256):
        hits = flag(wanted[start : start + 256] == iota((256, rows), 1))
        out_ref[pl.ds(start, 256), :] = nn(hits, table_ref[...]).astype(BF16)


def wanted_row(asked_ref):
    shards, capacity = asked_ref.shape
    slots = shards * capacity
    high, low = halves(asked_ref[...])
    column = flag(iota((capacity, slots), 0) == iota((capacity, slots), 1) % capacity)
    spread = nn(high, column) * 64.0 + nn(low, column)
    mine = iota((shards, slots), 0) == iota((shards, slots), 1) // capacity
    return jnp.sum(jnp.where(mine, spread, 0.0), axis=0, keepdims=True).astype(jnp.int32) - 1


def dense_kernel(asked_ref, asked_other_ref, got_ref, got_other_ref, after_ref, *out_refs):
    ring, (rows, _) = len(out_refs), out_refs[0].shape
    wanted = jnp.concatenate([wanted_row(asked_ref), wanted_row(asked_other_ref)], axis=1)
    got = jnp.concatenate([got_ref[...], got_other_ref[...]], axis=0)
    rank = lax.axis_index("dp")
    core, place = lax.rem(rank, 2), lax.div(rank, 2)
    places = iota((rows, wanted.shape[1]), 0)
    for d in (2, 3, 1, 0):
        ahead = lax.rem(jnp.where(core == 0, place + d, place + ring - d), ring)
        hits = flag(wanted - (ahead * 2 + core) * rows == places)
        out_refs[d][...] = nn(hits, got).astype(BF16)


def sigmoid(values):
    return 0.5 * jnp.tanh(0.5 * values) + 0.5


def centered_norm(values):
    centered = values - jnp.mean(values, axis=-1, keepdims=True)
    inverse = lax.rsqrt(jnp.mean(centered * centered, axis=-1, keepdims=True) + NORM_EPS)
    return centered * inverse, inverse


def norm_slope(grads, normed, inverse):
    return inverse * (
        grads
        - jnp.mean(grads, axis=-1, keepdims=True)
        - normed * jnp.mean(grads * normed, axis=-1, keepdims=True)
    )


def layer_kernel(
    lengths_ref, returned_ref, placed_ref, upstream_ref, w_proj_ref, w_out_ref, gain_ref,
    layer_ref, sent_ref, keep_ref, give_ref, slope_ref, acted_ref, grad_pre_ref,
    left_ref,
):
    slots = returned_ref.shape[0]
    tokens, width = upstream_ref.shape
    inner = w_out_ref.shape[0]
    placed = placed_ref[...]
    eye = iota((tokens, tokens), 0) == iota((tokens, tokens), 1)
    placed_col = jnp.sum(jnp.where(eye, placed, 0), axis=1, keepdims=True)
    inputs = nn(flag(placed_col == iota((tokens, slots), 1)), returned_ref[...])
    gain = gain_ref[...]
    hat, inverse = centered_norm(inputs)
    normed = (hat * gain).astype(BF16)
    for block in range(4):
        cols = pl.ds(block * inner, inner)
        pre = nn(normed, w_proj_ref[:, cols])
        sig = sigmoid(pre)
        acted_ref[:, cols] = (pre * sig).astype(BF16)
        slope_ref[:, cols] = sig * (1.0 + pre * (1.0 - sig))
    query_pos = iota((tokens, tokens), 0)
    key_pos = iota((tokens, tokens), 1)
    start_of = jnp.zeros((tokens, 1), jnp.int32)
    query_col = iota((tokens, 1), 0)
    end = jnp.int32(0)
    for i in range(lengths_ref.shape[1]):
        end = end + lengths_ref[0, i]
        start_of = jnp.where(query_col >= end, end, start_of)
    allowed = (key_pos <= query_pos) & (key_pos >= start_of)
    scale = HEAD_DIM ** (-0.5)

    def head(block, h):
        return acted_ref[:, pl.ds(block * inner + h * HEAD_DIM, HEAD_DIM)]

    mixed, weights, slopes = [], [], []
    for h in range(HEADS):
        scores = nt(head(2, h), head(3, h)) * scale
        sig = sigmoid(scores)
        weight = jnp.where(allowed, scores * sig, 0.0).astype(BF16)
        slopes.append(jnp.where(allowed, sig * (1.0 + scores * (1.0 - sig)), 0.0))
        weights.append(weight)
        mixed.append(nn(weight, head(1, h)))
    mixed_hat, mixed_inverse = centered_norm(jnp.concatenate(mixed, axis=1))
    gate = acted_ref[:, pl.ds(0, inner)].astype(F32)
    gated = (mixed_hat * gate).astype(BF16)
    layer_ref[...] = (inputs + nn(gated, w_out_ref[...])).astype(BF16)
    upstream = upstream_ref[...]
    grad_gated = nt(upstream, w_out_ref[...])
    grad_mixed = norm_slope(grad_gated * gate, mixed_hat, mixed_inverse).astype(BF16)

    def put(block, h, value):
        cols = pl.ds(block * inner + h * HEAD_DIM, HEAD_DIM)
        grad_pre_ref[:, cols] = (value * slope_ref[:, cols]).astype(BF16)

    grad_pre_ref[:, pl.ds(0, inner)] = (
        grad_gated * mixed_hat * slope_ref[:, pl.ds(0, inner)]
    ).astype(BF16)
    for h in range(HEADS):
        part = grad_mixed[:, h * HEAD_DIM : (h + 1) * HEAD_DIM]
        grad_scores = (nt(part, head(1, h)) * slopes[h] * scale).astype(BF16)
        put(1, h, tn(weights[h], part))
        put(2, h, nn(grad_scores, head(3, h)))
        put(3, h, tn(grad_scores, head(2, h)))
    grad_normed = nt(grad_pre_ref[...], w_proj_ref[...])
    grad_gain = jnp.sum(grad_normed * hat, axis=0, keepdims=True)
    row_grads = (
        upstream.astype(F32) + norm_slope(grad_normed * gain, hat, inverse)
    ).astype(BF16)
    sent_ref[...] = nn(flag(placed == iota((slots, tokens), 0)), row_grads).astype(BF16)

    half = keep_ref.shape[0] - 16
    core = lax.rem(lax.axis_index("dp"), 2)
    rows = width // 2
    left_ref[0] = normed.T
    left_ref[1] = gated.T
    blocks = (4 * inner + width) // LANES
    for out_ref, side in ((give_ref, 1 - core), (keep_ref, core)):
        first = pl.multiple_of(side * rows, rows)
        left = left_ref[0, pl.ds(first, rows), :]
        value = nn(left, grad_pre_ref[...])
        for b in range(4 * inner // LANES):
            for p in range(4):
                out_ref[pl.ds((p * blocks + b) * STRIP, STRIP), :] = value[
                    p * STRIP : (p + 1) * STRIP, b * LANES : (b + 1) * LANES
                ].astype(BF16)
        value = nn(left_ref[1, pl.ds(first, rows), :], upstream)
        for b in range(width // LANES):
            for p in range(4):
                at = (p * blocks + b + 4 * inner // LANES) * STRIP
                out_ref[pl.ds(at, STRIP), :] = value[
                    p * STRIP : (p + 1) * STRIP, b * LANES : (b + 1) * LANES
                ].astype(BF16)
    tail = gain_tail(
        jnp.concatenate(
            [grad_gain[:, k * LANES : (k + 1) * LANES] for k in range(width // LANES)], axis=0
        )
    )
    keep_ref[pl.ds(half, 16), :] = tail
    give_ref[pl.ds(half, 16), :] = tail


def gain_tail(grad_gain):
    high = grad_gain.astype(BF16).astype(F32)
    low = grad_gain - high
    return jnp.concatenate([high, low, jnp.zeros((8, LANES), F32)], axis=0).astype(BF16)


def first_place():
    rank = lax.axis_index("dp")
    along_x = lax.rem(lax.axis_index("table"), XS)
    along_y = lax.div(rank, 2)
    core = lax.rem(rank, 2)
    return core, jnp.where(core == 0, along_x, along_y), jnp.where(core == 0, along_y, along_x)


def part_sum(refs, start, count):
    value = refs[0][pl.ds(start, count), :].astype(F32)
    for ref in refs[1:]:
        value = value + ref[pl.ds(start, count), :].astype(F32)
    return value


def tail_sum(refs, rows):
    tail = part_sum(refs, rows, 16)
    return gain_tail(tail[0:4] + tail[4:8])


def turned_merge_kernel(mine_ref, other_ref, *out_refs):
    refs = (mine_ref, other_ref)
    chunk = out_refs[0].shape[0] - 16
    ring = len(out_refs)
    tail = tail_sum(refs, ring * chunk)
    _, place, _ = first_place()
    for d in (1, 2, 3, 0):
        start = pl.multiple_of(lax.rem(place + d, ring) * chunk, chunk)
        out_refs[d][pl.ds(0, chunk), :] = part_sum(refs, start, chunk).astype(BF16)
        out_refs[d][pl.ds(chunk, 16), :] = tail


def narrow_merge_kernel(*refs):
    refs, out_ref = refs[:-1], refs[-1]
    pieces, size, _ = out_ref.shape
    chunk = size - 8
    tail = tail_sum(refs, pieces * chunk).astype(F32)[0:8]
    for p in range(0, pieces, 2):
        two = part_sum(refs, p * chunk, 2 * chunk)
        for k in range(2):
            piece = jnp.concatenate([two[k * chunk : (k + 1) * chunk], tail], axis=0)
            out_ref[p + k] = piece.astype(BF16)


def turn_kernel(in_ref, near_ref, passed_ref, sum_ref, spread_ref, gain_ref):
    sum_ref[...] = (near_ref[...].astype(F32) + passed_ref[...].astype(F32)).astype(BF16)
    total = jnp.sum(in_ref[...].astype(F32), axis=0)
    rows = spread_ref.shape[1]
    mine = total[0:rows].astype(BF16)
    for p in range(spread_ref.shape[0]):
        spread_ref[p] = mine
    gain = total[rows : rows + 4] + total[rows + 4 : rows + 8]
    scale = lax.rsqrt(jnp.sum(gain * gain) / gain.size + STEP_EPS)
    gain_ref[...] = gain * scale


def finish_kernel(*refs):
    own_ref, near_ref, far_ref = refs[:3]
    pieces = refs[3:-6]
    table_ref, proj_ref, out_ref, sum_ref, stage_ref, sems = refs[-6:]
    sum_ref[...] = (
        own_ref[...].astype(F32) + near_ref[...].astype(F32) + far_ref[...].astype(F32)
    )
    copies = [pltpu.make_async_copy(sum_ref, table_ref, sems.at[len(pieces), 0])]
    copies[0].start()
    split = proj_ref.shape[1]
    blocks = stage_ref.shape[2] // LANES
    ring = len(pieces) // 2
    core, mine, other = first_place()

    def strip(piece, b):
        return piece[pl.ds(b * STRIP, STRIP), :].astype(F32)

    proj_sum = jnp.zeros((8, LANES), F32)
    out_sum = jnp.zeros((8, LANES), F32)
    for piece in pieces:
        for b in range(blocks):
            value = strip(piece, b)
            part = jnp.sum((value * value).reshape(STRIP // 8, 8, LANES), axis=0)
            if b * LANES < split:
                proj_sum = proj_sum + part
            else:
                out_sum = out_sum + part
    proj_scale = lax.rsqrt(jnp.sum(proj_sum) / proj_ref.size + STEP_EPS)
    out_scale = lax.rsqrt(jnp.sum(out_sum) / out_ref.size + STEP_EPS)
    for i, piece in enumerate(pieces):
        for b in range(blocks):
            scale = proj_scale if b * LANES < split else out_scale
            stage_ref[i, :, pl.ds(b * LANES, LANES)] = (strip(piece, b) * scale).astype(BF16)
        side, place = (core, mine) if i < ring else (1 - core, other)
        spot = side * ring + lax.rem(place + (ring - i % ring), ring)
        rows = pl.ds(pl.multiple_of(spot * STRIP, STRIP), STRIP)
        for k, (first, count, ref) in enumerate(
            ((0, split, proj_ref), (split, out_ref.shape[1], out_ref))
        ):
            copy = pltpu.make_async_copy(
                stage_ref.at[i, :, pl.ds(first, count)], ref.at[rows, :], sems.at[i, k]
            )
            copy.start()
            copies.append(copy)
    for copy in copies:
        copy.wait()


def hold_kernel(value_ref, near_ref, far_ref, out_ref):
    pass


ZS, XS, YS = 8, 4, 4


def device(z, x, y, c):
    return (z * XS + x) * (2 * YS) + y * 2 + c


PLACES = [(z, x, y, c) for z in range(ZS) for x in range(XS) for y in range(YS) for c in range(2)]
CORE_PERM = [(device(z, x, y, c), device(z, x, y, 1 - c)) for z, x, y, c in PLACES]


def first_perm(d):
    return [
        (
            device(z, x, y, c),
            device(z, (x + d) % XS, y, c) if c == 0 else device(z, x, (y + d) % YS, c),
        )
        for z, x, y, c in PLACES
    ]


def ring_perm(step):
    return [
        (device(z, x, y, c), device(z, x, (y + (step if c == 0 else -step)) % YS, c))
        for z, x, y, c in PLACES
    ]


SECOND_GROUPS = [
    [device(z, x, y, 0) for y in range(YS) for z in range(ZS)] for x in range(XS)
] + [[device(z, x, y, 1) for x in range(XS) for z in range(ZS)] for y in range(YS)]


def swap(values, groups):
    return lax.all_to_all(
        values, BOTH, split_axis=0, concat_axis=0, tiled=True, axis_index_groups=groups
    )


def body(table_rows, item_shard, item_slot, seq_lengths, cotangent, w_proj, w_out, norm_gain):
    shards = lax.axis_size("table")
    tokens = item_slot.shape[1]
    width = table_rows.shape[1]
    inner = w_out.shape[0]
    capacity = 2 * tokens // shards
    slots = shards * capacity
    requests, placed = call(
        functools.partial(request_kernel, table_rows.shape[0]),
        [shape((shards, capacity), jnp.int32), shape((1, tokens), jnp.int32)],
        item_shard.reshape(1, tokens) * table_rows.shape[0] + item_slot,
        flops=4 * slots * width * table_rows.shape[0],
    )
    asked = lax.all_to_all(requests, "table", split_axis=0, concat_axis=0, tiled=True)
    (picked,) = call(
        pick_kernel,
        [shape((slots, width), BF16)],
        asked,
        table_rows,
        flops=2 * slots * width * table_rows.shape[0],
    )
    returned = lax.all_to_all(
        picked.reshape(shards, capacity, width), "table", split_axis=0, concat_axis=0, tiled=True
    ).reshape(slots, width)
    half = width * (4 * inner + width) // (2 * LANES)
    grad_half = shape((half + 16, LANES), BF16)
    layer_rows, sent, keep, give = call(
        layer_kernel,
        [
            shape((tokens, width), BF16),
            shape((slots, width), BF16),
            grad_half,
            grad_half,
        ],
        seq_lengths[0],
        returned,
        placed,
        cotangent[0],
        w_proj,
        w_out,
        norm_gain.reshape(1, width),
        specs=[SMEM] + [VMEM] * 6,
        flops=6 * tokens * width * (4 * inner + width),
        transcendentals=tokens * (4 * inner + HEADS * tokens),
        scratch=[
            pltpu.VMEM((tokens, 4 * inner), F32),
            pltpu.VMEM((tokens, 4 * inner), BF16),
            pltpu.VMEM((tokens, 4 * inner), BF16),
            pltpu.VMEM((2, width, tokens), BF16),
        ],
    )
    got = lax.all_to_all(
        sent.reshape(shards, capacity, width), "table", split_axis=0, concat_axis=0, tiled=True
    ).reshape(slots, width)
    rows = table_rows.shape[0] // (2 * YS)
    other = lax.ppermute(give, BOTH, CORE_PERM)
    parts = call(turned_merge_kernel, [shape((half // 4 + 16, LANES), BF16)] * 4, keep, other)
    parts = [parts[0]] + [lax.ppermute(parts[d], BOTH, first_perm(d)) for d in (1, 2, 3)]
    (grads,) = call(narrow_merge_kernel, [shape((32, half // 128 + 8, LANES), BF16)], *parts)
    own, near, two, far = call(
        dense_kernel,
        [shape((rows, width), BF16)] * YS,
        asked,
        lax.ppermute(asked, BOTH, CORE_PERM),
        got,
        lax.ppermute(got, BOTH, CORE_PERM),
        grads,
        specs=[VMEM] * 4 + [ANY],
        flops=2 * slots * width * table_rows.shape[0],
    )
    passed = lax.ppermute(two, BOTH, ring_perm(1))
    far = lax.ppermute(far, BOTH, ring_perm(-1))
    grads = swap(grads, SECOND_GROUPS)
    near, grads, step_gain = call(
        turn_kernel,
        [
            shape((rows, width), BF16),
            shape((32, half // 128, LANES), BF16),
            shape((width // LANES, LANES), F32),
        ],
        grads,
        near,
        passed,
    )
    near = lax.ppermute(near, BOTH, ring_perm(1))
    grads = swap(grads, SECOND_GROUPS).reshape(half // 4, LANES)
    (grads,) = call(
        hold_kernel,
        [shape(grads.shape, BF16)],
        grads,
        near,
        far,
        specs=[ANY] * 3,
        out_specs=[ANY],
        aliases={0: 0},
    )
    mine = [grads] + [lax.ppermute(grads, BOTH, first_perm(d)) for d in (1, 2, 3)]
    others = [lax.ppermute(piece, BOTH, CORE_PERM) for piece in mine]
    table_grad, step_proj, step_out = call(
        finish_kernel,
        [shape((rows, width), F32), shape(w_proj.shape, BF16), shape(w_out.shape, BF16)],
        own,
        near,
        far,
        *mine,
        *others,
        out_specs=[HBM, HBM, HBM],
        scratch=[
            pltpu.VMEM((rows, width), F32),
            pltpu.VMEM((8, STRIP, 4 * inner + width), BF16),
            pltpu.SemaphoreType.DMA((9, 2)),
        ],
    )
    return (layer_rows[None], table_grad, step_proj, step_out, step_gain.reshape(width))


def solution(mesh):
    placed = (
        P("table", None),
        P("dp", "table", None),
        P("dp", "table"),
        P("dp", "table", None),
        P("dp", "table", None),
        P(),
        P(),
        P(),
    )
    return jax.shard_map(
        body,
        mesh=mesh,
        in_specs=placed,
        out_specs=(P("dp", "table", None), P(("table", "dp"), None), P(), P(), P()),
        check_vma=False,
    )
```

```python
import functools

import jax
import jax.numpy as jnp
from jax import lax
from jax.experimental import pallas as pl
from jax.experimental.pallas import tpu as pltpu
from jax.sharding import PartitionSpec as P

HEADS = 4
HEAD_DIM = 128
NORM_EPS = 1e-05
STEP_EPS = 1e-06
BOTH = ("table", "dp")
F32 = jnp.float32
BF16 = jnp.bfloat16
LANES = 128
STRIP = 64
VMEM = pl.BlockSpec(memory_space=pltpu.VMEM)
SMEM = pl.BlockSpec(memory_space=pltpu.SMEM)
ANY = pl.BlockSpec(memory_space=pl.ANY)
HBM = pl.BlockSpec(memory_space=pltpu.HBM)


def call(
    kernel, outs, *operands, specs=None, out_specs=None, flops=0, transcendentals=0, scratch=(),
    aliases=None,
):
    moved = sum(v.size * v.dtype.itemsize for v in operands)
    moved += sum(v.size * v.dtype.itemsize for v in outs)
    return pl.pallas_call(
        kernel,
        out_shape=outs,
        in_specs=specs if specs is not None else [VMEM] * len(operands),
        out_specs=out_specs if out_specs is not None else [VMEM] * len(outs),
        scratch_shapes=list(scratch),
        input_output_aliases=aliases or {},
        cost_estimate=pl.CostEstimate(
            flops=flops, bytes_accessed=moved, transcendentals=transcendentals
        ),
        compiler_params=pltpu.CompilerParams(vmem_limit_bytes=40 * 1024 * 1024),
    )(*operands)


def shape(dims, dtype):
    return jax.ShapeDtypeStruct(dims, dtype)


def nn(a, b):
    return jnp.dot(a, b, preferred_element_type=F32)


def nt(a, b):
    return lax.dot_general(a, b, (((1,), (1,)), ((), ())), preferred_element_type=F32)


def tn(a, b):
    return lax.dot_general(a, b, (((0,), (0,)), ((), ())), preferred_element_type=F32)


def iota(dims, axis):
    return lax.broadcasted_iota(jnp.int32, dims, axis)


def flag(mask):
    return jnp.where(mask, 1.0, 0.0).astype(BF16)


def request_kernel(rows, item_ref, request_ref, placed_ref):
    shards, capacity = request_ref.shape
    tokens = item_ref.shape[1]
    item = item_ref[...]
    target = item // rows
    named = target == iota((shards, tokens), 0)
    earlier = flag(iota((tokens, tokens), 0) < iota((tokens, tokens), 1))
    counts = nn(flag(named), earlier)
    rank = jnp.sum(jnp.where(named, counts, 0.0), axis=0, keepdims=True).astype(jnp.int32)
    placed_ref[...] = target * capacity + rank
    wanted = item - target * rows + 1
    at_rank = rank == iota((capacity, tokens), 0)
    high = jnp.where(at_rank, wanted // 64, 0).astype(F32).astype(BF16)
    low = jnp.where(at_rank, wanted % 64, 0).astype(F32).astype(BF16)
    picked = nt(flag(named), high) * 64.0 + nt(flag(named), low)
    request_ref[...] = picked.astype(jnp.int32) - 1


def halves(values):
    shifted = values + 1
    high = (shifted // 64).astype(F32).astype(BF16)
    low = (shifted % 64).astype(F32).astype(BF16)
    return high, low


def pick_kernel(asked_ref, table_ref, out_ref):
    shards, capacity = asked_ref.shape
    slots = shards * capacity
    rows = table_ref.shape[0]
    high, low = halves(asked_ref[...])
    owner = flag(iota((slots, shards), 0) // capacity == iota((slots, shards), 1))
    spread = nn(owner, high) * 64.0 + nn(owner, low)
    mine = iota((slots, capacity), 0) % capacity == iota((slots, capacity), 1)
    wanted = jnp.sum(jnp.where(mine, spread, 0.0), axis=1, keepdims=True).astype(jnp.int32) - 1
    for start in range(0, slots, 256):
        hits = flag(wanted[start : start + 256] == iota((256, rows), 1))
        out_ref[pl.ds(start, 256), :] = nn(hits, table_ref[...]).astype(BF16)


def wanted_row(asked_ref):
    shards, capacity = asked_ref.shape
    slots = shards * capacity
    high, low = halves(asked_ref[...])
    column = flag(iota((capacity, slots), 0) == iota((capacity, slots), 1) % capacity)
    spread = nn(high, column) * 64.0 + nn(low, column)
    mine = iota((shards, slots), 0) == iota((shards, slots), 1) // capacity
    return jnp.sum(jnp.where(mine, spread, 0.0), axis=0, keepdims=True).astype(jnp.int32) - 1


def dense_kernel(asked_ref, asked_other_ref, got_ref, got_other_ref, after_ref, *out_refs):
    ring, (rows, _) = len(out_refs), out_refs[0].shape
    wanted = jnp.concatenate([wanted_row(asked_ref), wanted_row(asked_other_ref)], axis=1)
    got = jnp.concatenate([got_ref[...], got_other_ref[...]], axis=0)
    rank = lax.axis_index("dp")
    core, place = lax.rem(rank, 2), lax.div(rank, 2)
    places = iota((rows, wanted.shape[1]), 0)
    for d in (2, 3, 1, 0):
        ahead = lax.rem(jnp.where(core == 0, place + d, place + ring - d), ring)
        hits = flag(wanted - (ahead * 2 + core) * rows == places)
        out_refs[d][...] = nn(hits, got).astype(BF16)


def sigmoid(values):
    return 0.5 * jnp.tanh(0.5 * values) + 0.5


def centered_norm(values):
    centered = values - jnp.mean(values, axis=-1, keepdims=True)
    inverse = lax.rsqrt(jnp.mean(centered * centered, axis=-1, keepdims=True) + NORM_EPS)
    return centered * inverse, inverse


def norm_slope(grads, normed, inverse):
    return inverse * (
        grads
        - jnp.mean(grads, axis=-1, keepdims=True)
        - normed * jnp.mean(grads * normed, axis=-1, keepdims=True)
    )


def layer_kernel(
    lengths_ref, returned_ref, placed_ref, upstream_ref, w_proj_ref, w_out_ref, gain_ref,
    layer_ref, sent_ref, grad_pre_ref, left_ref, tail_ref, slope_ref, acted_ref,
):
    slots = returned_ref.shape[0]
    tokens, width = upstream_ref.shape
    inner = w_out_ref.shape[0]
    placed = placed_ref[...]
    eye = iota((tokens, tokens), 0) == iota((tokens, tokens), 1)
    placed_col = jnp.sum(jnp.where(eye, placed, 0), axis=1, keepdims=True)
    inputs = nn(flag(placed_col == iota((tokens, slots), 1)), returned_ref[...])
    gain = gain_ref[...]
    hat, inverse = centered_norm(inputs)
    normed = (hat * gain).astype(BF16)
    for block in range(4):
        cols = pl.ds(block * inner, inner)
        pre = nn(normed, w_proj_ref[:, cols])
        sig = sigmoid(pre)
        acted_ref[:, cols] = (pre * sig).astype(BF16)
        slope_ref[:, cols] = sig * (1.0 + pre * (1.0 - sig))
    query_pos = iota((tokens, tokens), 0)
    key_pos = iota((tokens, tokens), 1)
    start_of = jnp.zeros((tokens, 1), jnp.int32)
    query_col = iota((tokens, 1), 0)
    end = jnp.int32(0)
    for i in range(lengths_ref.shape[1]):
        end = end + lengths_ref[0, i]
        start_of = jnp.where(query_col >= end, end, start_of)
    allowed = (key_pos <= query_pos) & (key_pos >= start_of)
    scale = HEAD_DIM ** (-0.5)

    def head(block, h):
        return acted_ref[:, pl.ds(block * inner + h * HEAD_DIM, HEAD_DIM)]

    mixed, weights, slopes = [], [], []
    for h in range(HEADS):
        scores = nt(head(2, h), head(3, h)) * scale
        sig = sigmoid(scores)
        weight = jnp.where(allowed, scores * sig, 0.0).astype(BF16)
        slopes.append(jnp.where(allowed, sig * (1.0 + scores * (1.0 - sig)), 0.0))
        weights.append(weight)
        mixed.append(nn(weight, head(1, h)))
    mixed_hat, mixed_inverse = centered_norm(jnp.concatenate(mixed, axis=1))
    gate = acted_ref[:, pl.ds(0, inner)].astype(F32)
    gated = (mixed_hat * gate).astype(BF16)
    layer_ref[...] = (inputs + nn(gated, w_out_ref[...])).astype(BF16)
    upstream = upstream_ref[...]
    grad_gated = nt(upstream, w_out_ref[...])
    grad_mixed = norm_slope(grad_gated * gate, mixed_hat, mixed_inverse).astype(BF16)

    def put(block, h, value):
        cols = pl.ds(block * inner + h * HEAD_DIM, HEAD_DIM)
        grad_pre_ref[:, cols] = (value * slope_ref[:, cols]).astype(BF16)

    grad_pre_ref[:, pl.ds(0, inner)] = (
        grad_gated * mixed_hat * slope_ref[:, pl.ds(0, inner)]
    ).astype(BF16)
    for h in range(HEADS):
        part = grad_mixed[:, h * HEAD_DIM : (h + 1) * HEAD_DIM]
        grad_scores = (nt(part, head(1, h)) * slopes[h] * scale).astype(BF16)
        put(1, h, tn(weights[h], part))
        put(2, h, nn(grad_scores, head(3, h)))
        put(3, h, tn(grad_scores, head(2, h)))
    grad_normed = nt(grad_pre_ref[...], w_proj_ref[...])
    grad_gain = jnp.sum(grad_normed * hat, axis=0, keepdims=True)
    row_grads = (
        upstream.astype(F32) + norm_slope(grad_normed * gain, hat, inverse)
    ).astype(BF16)
    sent_ref[...] = nn(flag(placed == iota((slots, tokens), 0)), row_grads).astype(BF16)

    left_ref[0] = normed.T
    left_ref[1] = gated.T
    tail_ref[...] = gain_tail(
        jnp.concatenate(
            [grad_gain[:, k * LANES : (k + 1) * LANES] for k in range(width // LANES)], axis=0
        )
    )


def weights_kernel(left_ref, grad_pre_ref, upstream_ref, tail_ref, keep_ref, give_ref):
    width = upstream_ref.shape[1]
    inner = grad_pre_ref.shape[1] // 4
    half = keep_ref.shape[0] - 16
    core = lax.rem(lax.axis_index("dp"), 2)
    rows = width // 2
    blocks = (4 * inner + width) // LANES
    for out_ref, side in ((give_ref, 1 - core), (keep_ref, core)):
        out_ref[pl.ds(half, 16), :] = tail_ref[...]
        first = pl.multiple_of(side * rows, rows)
        left = left_ref[0, pl.ds(first, rows), :]
        value = nn(left, grad_pre_ref[...])
        for b in range(4 * inner // LANES):
            for p in range(4):
                out_ref[pl.ds((p * blocks + b) * STRIP, STRIP), :] = value[
                    p * STRIP : (p + 1) * STRIP, b * LANES : (b + 1) * LANES
                ].astype(BF16)
        value = nn(left_ref[1, pl.ds(first, rows), :], upstream_ref[...])
        for b in range(width // LANES):
            for p in range(4):
                at = (p * blocks + b + 4 * inner // LANES) * STRIP
                out_ref[pl.ds(at, STRIP), :] = value[
                    p * STRIP : (p + 1) * STRIP, b * LANES : (b + 1) * LANES
                ].astype(BF16)


def gain_tail(grad_gain):
    high = grad_gain.astype(BF16).astype(F32)
    low = grad_gain - high
    return jnp.concatenate([high, low, jnp.zeros((8, LANES), F32)], axis=0).astype(BF16)


def first_place():
    rank = lax.axis_index("dp")
    along_x = lax.rem(lax.axis_index("table"), XS)
    along_y = lax.div(rank, 2)
    core = lax.rem(rank, 2)
    return core, jnp.where(core == 0, along_x, along_y), jnp.where(core == 0, along_y, along_x)


def part_sum(refs, start, count):
    value = refs[0][pl.ds(start, count), :].astype(F32)
    for ref in refs[1:]:
        value = value + ref[pl.ds(start, count), :].astype(F32)
    return value


def tail_sum(refs, rows):
    tail = part_sum(refs, rows, 16)
    return gain_tail(tail[0:4] + tail[4:8])


def turned_merge_kernel(mine_ref, other_ref, *out_refs):
    refs = (mine_ref, other_ref)
    chunk = out_refs[0].shape[0] - 16
    ring = len(out_refs)
    tail = tail_sum(refs, ring * chunk)
    _, place, _ = first_place()
    for d in (1, 2, 3, 0):
        start = pl.multiple_of(lax.rem(place + d, ring) * chunk, chunk)
        out_refs[d][pl.ds(0, chunk), :] = part_sum(refs, start, chunk).astype(BF16)
        out_refs[d][pl.ds(chunk, 16), :] = tail


def narrow_merge_kernel(*refs):
    refs, out_ref = refs[:-1], refs[-1]
    pieces, size, _ = out_ref.shape
    chunk = size - 8
    tail = tail_sum(refs, pieces * chunk).astype(F32)[0:8]
    for p in range(0, pieces, 2):
        two = part_sum(refs, p * chunk, 2 * chunk)
        for k in range(2):
            piece = jnp.concatenate([two[k * chunk : (k + 1) * chunk], tail], axis=0)
            out_ref[p + k] = piece.astype(BF16)


def add_kernel(near_ref, passed_ref, after_ref, sum_ref):
    sum_ref[...] = (near_ref[...].astype(F32) + passed_ref[...].astype(F32)).astype(BF16)


def turn_kernel(in_ref, after_ref, spread_ref, gain_ref):
    total = jnp.sum(in_ref[...].astype(F32), axis=0)
    rows = spread_ref.shape[1]
    mine = total[0:rows].astype(BF16)
    for p in range(spread_ref.shape[0]):
        spread_ref[p] = mine
    gain = total[rows : rows + 4] + total[rows + 4 : rows + 8]
    scale = lax.rsqrt(jnp.sum(gain * gain) / gain.size + STEP_EPS)
    gain_ref[...] = gain * scale


def finish_kernel(*refs):
    own_ref, near_ref, far_ref = refs[:3]
    pieces = refs[3:-6]
    table_ref, proj_ref, out_ref, sum_ref, stage_ref, sems = refs[-6:]
    sum_ref[...] = (
        own_ref[...].astype(F32) + near_ref[...].astype(F32) + far_ref[...].astype(F32)
    )
    copies = [pltpu.make_async_copy(sum_ref, table_ref, sems.at[len(pieces), 0])]
    copies[0].start()
    split = proj_ref.shape[1]
    blocks = stage_ref.shape[2] // LANES
    ring = len(pieces) // 2
    core, mine, other = first_place()

    def strip(piece, b):
        return piece[pl.ds(b * STRIP, STRIP), :].astype(F32)

    proj_sum = jnp.zeros((8, LANES), F32)
    out_sum = jnp.zeros((8, LANES), F32)
    for piece in pieces:
        for b in range(blocks):
            value = strip(piece, b)
            part = jnp.sum((value * value).reshape(STRIP // 8, 8, LANES), axis=0)
            if b * LANES < split:
                proj_sum = proj_sum + part
            else:
                out_sum = out_sum + part
    proj_scale = lax.rsqrt(jnp.sum(proj_sum) / proj_ref.size + STEP_EPS)
    out_scale = lax.rsqrt(jnp.sum(out_sum) / out_ref.size + STEP_EPS)
    for i, piece in enumerate(pieces):
        for b in range(blocks):
            scale = proj_scale if b * LANES < split else out_scale
            stage_ref[i, :, pl.ds(b * LANES, LANES)] = (strip(piece, b) * scale).astype(BF16)
        side, place = (core, mine) if i < ring else (1 - core, other)
        spot = side * ring + lax.rem(place + (ring - i % ring), ring)
        rows = pl.ds(pl.multiple_of(spot * STRIP, STRIP), STRIP)
        for k, (first, count, ref) in enumerate(
            ((0, split, proj_ref), (split, out_ref.shape[1], out_ref))
        ):
            copy = pltpu.make_async_copy(
                stage_ref.at[i, :, pl.ds(first, count)], ref.at[rows, :], sems.at[i, k]
            )
            copy.start()
            copies.append(copy)
    for copy in copies:
        copy.wait()


def hold_kernel(value_ref, near_ref, far_ref, out_ref):
    pass


ZS, XS, YS = 8, 4, 4


def device(z, x, y, c):
    return (z * XS + x) * (2 * YS) + y * 2 + c


PLACES = [(z, x, y, c) for z in range(ZS) for x in range(XS) for y in range(YS) for c in range(2)]
CORE_PERM = [(device(z, x, y, c), device(z, x, y, 1 - c)) for z, x, y, c in PLACES]


def first_perm(d):
    return [
        (
            device(z, x, y, c),
            device(z, (x + d) % XS, y, c) if c == 0 else device(z, x, (y + d) % YS, c),
        )
        for z, x, y, c in PLACES
    ]


def ring_perm(step):
    return [
        (device(z, x, y, c), device(z, x, (y + (step if c == 0 else -step)) % YS, c))
        for z, x, y, c in PLACES
    ]


SECOND_GROUPS = [
    [device(z, x, y, 0) for y in range(YS) for z in range(ZS)] for x in range(XS)
] + [[device(z, x, y, 1) for x in range(XS) for z in range(ZS)] for y in range(YS)]


def swap(values, groups):
    return lax.all_to_all(
        values, BOTH, split_axis=0, concat_axis=0, tiled=True, axis_index_groups=groups
    )


def body(table_rows, item_shard, item_slot, seq_lengths, cotangent, w_proj, w_out, norm_gain):
    shards = lax.axis_size("table")
    tokens = item_slot.shape[1]
    width = table_rows.shape[1]
    inner = w_out.shape[0]
    capacity = 2 * tokens // shards
    slots = shards * capacity
    requests, placed = call(
        functools.partial(request_kernel, table_rows.shape[0]),
        [shape((shards, capacity), jnp.int32), shape((1, tokens), jnp.int32)],
        item_shard.reshape(1, tokens) * table_rows.shape[0] + item_slot,
        flops=4 * slots * width * table_rows.shape[0],
    )
    asked = lax.all_to_all(requests, "table", split_axis=0, concat_axis=0, tiled=True)
    (picked,) = call(
        pick_kernel,
        [shape((slots, width), BF16)],
        asked,
        table_rows,
        flops=2 * slots * width * table_rows.shape[0],
    )
    returned = lax.all_to_all(
        picked.reshape(shards, capacity, width), "table", split_axis=0, concat_axis=0, tiled=True
    ).reshape(slots, width)
    half = width * (4 * inner + width) // (2 * LANES)
    grad_half = shape((half + 16, LANES), BF16)
    layer_rows, sent, grad_pre, left, tail = call(
        layer_kernel,
        [
            shape((tokens, width), BF16),
            shape((slots, width), BF16),
            shape((tokens, 4 * inner), BF16),
            shape((2, width, tokens), BF16),
            shape((16, LANES), BF16),
        ],
        seq_lengths[0],
        returned,
        placed,
        cotangent[0],
        w_proj,
        w_out,
        norm_gain.reshape(1, width),
        specs=[SMEM] + [VMEM] * 6,
        flops=4 * tokens * width * (4 * inner + width),
        transcendentals=tokens * (4 * inner + HEADS * tokens),
        scratch=[
            pltpu.VMEM((tokens, 4 * inner), F32),
            pltpu.VMEM((tokens, 4 * inner), BF16),
        ],
    )
    keep, give = call(
        weights_kernel,
        [grad_half, grad_half],
        left,
        grad_pre,
        cotangent[0],
        tail,
        flops=2 * tokens * width * (4 * inner + width),
    )
    got = lax.all_to_all(
        sent.reshape(shards, capacity, width), "table", split_axis=0, concat_axis=0, tiled=True
    ).reshape(slots, width)
    rows = table_rows.shape[0] // (2 * YS)
    other = lax.ppermute(give, BOTH, CORE_PERM)
    parts = call(turned_merge_kernel, [shape((half // 4 + 16, LANES), BF16)] * 4, keep, other)
    parts = [parts[0]] + [lax.ppermute(parts[d], BOTH, first_perm(d)) for d in (1, 2, 3)]
    (grads,) = call(narrow_merge_kernel, [shape((32, half // 128 + 8, LANES), BF16)], *parts)
    own, near, two, far = call(
        dense_kernel,
        [shape((rows, width), BF16)] * YS,
        asked,
        lax.ppermute(asked, BOTH, CORE_PERM),
        got,
        lax.ppermute(got, BOTH, CORE_PERM),
        grads,
        specs=[VMEM] * 4 + [ANY],
        flops=2 * slots * width * table_rows.shape[0],
    )
    passed = lax.ppermute(two, BOTH, ring_perm(1))
    far = lax.ppermute(far, BOTH, ring_perm(-1))
    grads = swap(grads, SECOND_GROUPS)
    grads, step_gain = call(
        turn_kernel,
        [shape((32, half // 128, LANES), BF16), shape((width // LANES, LANES), F32)],
        grads,
        near,
        specs=[VMEM, ANY],
    )
    (near,) = call(
        add_kernel,
        [shape((rows, width), BF16)],
        near,
        passed,
        grads,
        specs=[VMEM, VMEM, ANY],
    )
    near_sum = near
    near = lax.ppermute(near_sum, BOTH, ring_perm(1))
    grads = swap(grads, SECOND_GROUPS).reshape(half // 4, LANES)
    (grads,) = call(
        hold_kernel,
        [shape(grads.shape, BF16)],
        grads,
        near_sum,
        far,
        specs=[ANY] * 3,
        out_specs=[ANY],
        aliases={0: 0},
    )
    mine = [grads] + [lax.ppermute(grads, BOTH, first_perm(d)) for d in (1, 2, 3)]
    (mine[1],) = call(
        hold_kernel,
        [shape(grads.shape, BF16)],
        mine[1],
        near,
        far,
        specs=[ANY] * 3,
        out_specs=[ANY],
        aliases={0: 0},
    )
    others = [lax.ppermute(piece, BOTH, CORE_PERM) for piece in mine]
    table_grad, step_proj, step_out = call(
        finish_kernel,
        [shape((rows, width), F32), shape(w_proj.shape, BF16), shape(w_out.shape, BF16)],
        own,
        near,
        far,
        *mine,
        *others,
        out_specs=[HBM, HBM, HBM],
        scratch=[
            pltpu.VMEM((rows, width), F32),
            pltpu.VMEM((8, STRIP, 4 * inner + width), BF16),
            pltpu.SemaphoreType.DMA((9, 2)),
        ],
    )
    return (layer_rows[None], table_grad, step_proj, step_out, step_gain.reshape(width))


def solution(mesh):
    placed = (
        P("table", None),
        P("dp", "table", None),
        P("dp", "table"),
        P("dp", "table", None),
        P("dp", "table", None),
        P(),
        P(),
        P(),
    )
    return jax.shard_map(
        body,
        mesh=mesh,
        in_specs=placed,
        out_specs=(P("dp", "table", None), P(("table", "dp"), None), P(), P(), P()),
        check_vma=False,
    )
```

```python
import functools

import jax
import jax.numpy as jnp
from jax import lax
from jax.experimental import pallas as pl
from jax.experimental.pallas import tpu as pltpu
from jax.sharding import PartitionSpec as P

HEADS = 4
HEAD_DIM = 128
NORM_EPS = 1e-05
STEP_EPS = 1e-06
BOTH = ("table", "dp")
F32 = jnp.float32
BF16 = jnp.bfloat16
LANES = 128
STRIP = 64
VMEM = pl.BlockSpec(memory_space=pltpu.VMEM)
SMEM = pl.BlockSpec(memory_space=pltpu.SMEM)
ANY = pl.BlockSpec(memory_space=pl.ANY)
HBM = pl.BlockSpec(memory_space=pltpu.HBM)


def call(
    kernel, outs, *operands, specs=None, out_specs=None, flops=0, transcendentals=0, scratch=(),
    aliases=None,
):
    moved = sum(v.size * v.dtype.itemsize for v in operands)
    moved += sum(v.size * v.dtype.itemsize for v in outs)
    return pl.pallas_call(
        kernel,
        out_shape=outs,
        in_specs=specs if specs is not None else [VMEM] * len(operands),
        out_specs=out_specs if out_specs is not None else [VMEM] * len(outs),
        scratch_shapes=list(scratch),
        input_output_aliases=aliases or {},
        cost_estimate=pl.CostEstimate(
            flops=flops, bytes_accessed=moved, transcendentals=transcendentals
        ),
        compiler_params=pltpu.CompilerParams(vmem_limit_bytes=40 * 1024 * 1024),
    )(*operands)


def shape(dims, dtype):
    return jax.ShapeDtypeStruct(dims, dtype)


def nn(a, b):
    return jnp.dot(a, b, preferred_element_type=F32)


def nt(a, b):
    return lax.dot_general(a, b, (((1,), (1,)), ((), ())), preferred_element_type=F32)


def tn(a, b):
    return lax.dot_general(a, b, (((0,), (0,)), ((), ())), preferred_element_type=F32)


def iota(dims, axis):
    return lax.broadcasted_iota(jnp.int32, dims, axis)


def flag(mask):
    return jnp.where(mask, 1.0, 0.0).astype(BF16)


def request_kernel(rows, item_ref, request_ref, placed_ref):
    shards, capacity = request_ref.shape
    tokens = item_ref.shape[1]
    item = item_ref[...]
    target = item // rows
    named = target == iota((shards, tokens), 0)
    earlier = flag(iota((tokens, tokens), 0) < iota((tokens, tokens), 1))
    counts = nn(flag(named), earlier)
    rank = jnp.sum(jnp.where(named, counts, 0.0), axis=0, keepdims=True).astype(jnp.int32)
    placed_ref[...] = target * capacity + rank
    wanted = item - target * rows + 1
    at_rank = rank == iota((capacity, tokens), 0)
    high = jnp.where(at_rank, wanted // 64, 0).astype(F32).astype(BF16)
    low = jnp.where(at_rank, wanted % 64, 0).astype(F32).astype(BF16)
    picked = nt(flag(named), high) * 64.0 + nt(flag(named), low)
    request_ref[...] = picked.astype(jnp.int32) - 1


def halves(values):
    shifted = values + 1
    high = (shifted // 64).astype(F32).astype(BF16)
    low = (shifted % 64).astype(F32).astype(BF16)
    return high, low


def pick_kernel(asked_ref, table_ref, out_ref):
    shards, capacity = asked_ref.shape
    slots = shards * capacity
    rows = table_ref.shape[0]
    high, low = halves(asked_ref[...])
    owner = flag(iota((slots, shards), 0) // capacity == iota((slots, shards), 1))
    spread = nn(owner, high) * 64.0 + nn(owner, low)
    mine = iota((slots, capacity), 0) % capacity == iota((slots, capacity), 1)
    wanted = jnp.sum(jnp.where(mine, spread, 0.0), axis=1, keepdims=True).astype(jnp.int32) - 1
    for start in range(0, slots, 256):
        hits = flag(wanted[start : start + 256] == iota((256, rows), 1))
        out_ref[pl.ds(start, 256), :] = nn(hits, table_ref[...]).astype(BF16)


def wanted_row(asked_ref):
    shards, capacity = asked_ref.shape
    slots = shards * capacity
    high, low = halves(asked_ref[...])
    column = flag(iota((capacity, slots), 0) == iota((capacity, slots), 1) % capacity)
    spread = nn(high, column) * 64.0 + nn(low, column)
    mine = iota((shards, slots), 0) == iota((shards, slots), 1) // capacity
    return jnp.sum(jnp.where(mine, spread, 0.0), axis=0, keepdims=True).astype(jnp.int32) - 1


def dense_kernel(asked_ref, asked_other_ref, got_ref, got_other_ref, after_ref, *out_refs):
    ring, (rows, _) = len(out_refs), out_refs[0].shape
    wanted = jnp.concatenate([wanted_row(asked_ref), wanted_row(asked_other_ref)], axis=1)
    got = jnp.concatenate([got_ref[...], got_other_ref[...]], axis=0)
    rank = lax.axis_index("dp")
    core, place = lax.rem(rank, 2), lax.div(rank, 2)
    places = iota((rows, wanted.shape[1]), 0)
    for d in (2, 3, 1, 0):
        ahead = lax.rem(jnp.where(core == 0, place + d, place + ring - d), ring)
        hits = flag(wanted - (ahead * 2 + core) * rows == places)
        out_refs[d][...] = nn(hits, got).astype(BF16)


def sigmoid(values):
    return 0.5 * jnp.tanh(0.5 * values) + 0.5


def centered_norm(values):
    centered = values - jnp.mean(values, axis=-1, keepdims=True)
    inverse = lax.rsqrt(jnp.mean(centered * centered, axis=-1, keepdims=True) + NORM_EPS)
    return centered * inverse, inverse


def norm_slope(grads, normed, inverse):
    return inverse * (
        grads
        - jnp.mean(grads, axis=-1, keepdims=True)
        - normed * jnp.mean(grads * normed, axis=-1, keepdims=True)
    )


def layer_kernel(
    lengths_ref, returned_ref, placed_ref, upstream_ref, w_proj_ref, w_out_ref, gain_ref,
    layer_ref, sent_ref, grad_pre_ref, left_ref, tail_ref, slope_ref, acted_ref,
):
    slots = returned_ref.shape[0]
    tokens, width = upstream_ref.shape
    inner = w_out_ref.shape[0]
    placed = placed_ref[...]
    eye = iota((tokens, tokens), 0) == iota((tokens, tokens), 1)
    placed_col = jnp.sum(jnp.where(eye, placed, 0), axis=1, keepdims=True)
    inputs = nn(flag(placed_col == iota((tokens, slots), 1)), returned_ref[...])
    gain = gain_ref[...]
    hat, inverse = centered_norm(inputs)
    normed = (hat * gain).astype(BF16)
    for block in range(4):
        cols = pl.ds(block * inner, inner)
        pre = nn(normed, w_proj_ref[:, cols])
        sig = sigmoid(pre)
        acted_ref[:, cols] = (pre * sig).astype(BF16)
        slope_ref[:, cols] = sig * (1.0 + pre * (1.0 - sig))
    query_pos = iota((tokens, tokens), 0)
    key_pos = iota((tokens, tokens), 1)
    start_of = jnp.zeros((tokens, 1), jnp.int32)
    query_col = iota((tokens, 1), 0)
    end = jnp.int32(0)
    for i in range(lengths_ref.shape[1]):
        end = end + lengths_ref[0, i]
        start_of = jnp.where(query_col >= end, end, start_of)
    allowed = (key_pos <= query_pos) & (key_pos >= start_of)
    scale = HEAD_DIM ** (-0.5)

    def head(block, h):
        return acted_ref[:, pl.ds(block * inner + h * HEAD_DIM, HEAD_DIM)]

    mixed, weights, slopes = [], [], []
    for h in range(HEADS):
        scores = nt(head(2, h), head(3, h)) * scale
        sig = sigmoid(scores)
        weight = jnp.where(allowed, scores * sig, 0.0).astype(BF16)
        slopes.append(jnp.where(allowed, sig * (1.0 + scores * (1.0 - sig)), 0.0))
        weights.append(weight)
        mixed.append(nn(weight, head(1, h)))
    mixed_hat, mixed_inverse = centered_norm(jnp.concatenate(mixed, axis=1))
    gate = acted_ref[:, pl.ds(0, inner)].astype(F32)
    gated = (mixed_hat * gate).astype(BF16)
    layer_ref[...] = (inputs + nn(gated, w_out_ref[...])).astype(BF16)
    upstream = upstream_ref[...]
    grad_gated = nt(upstream, w_out_ref[...])
    grad_mixed = norm_slope(grad_gated * gate, mixed_hat, mixed_inverse).astype(BF16)

    def put(block, h, value):
        cols = pl.ds(block * inner + h * HEAD_DIM, HEAD_DIM)
        grad_pre_ref[:, cols] = (value * slope_ref[:, cols]).astype(BF16)

    grad_pre_ref[:, pl.ds(0, inner)] = (
        grad_gated * mixed_hat * slope_ref[:, pl.ds(0, inner)]
    ).astype(BF16)
    for h in range(HEADS):
        part = grad_mixed[:, h * HEAD_DIM : (h + 1) * HEAD_DIM]
        grad_scores = (nt(part, head(1, h)) * slopes[h] * scale).astype(BF16)
        put(1, h, tn(weights[h], part))
        put(2, h, nn(grad_scores, head(3, h)))
        put(3, h, tn(grad_scores, head(2, h)))
    grad_normed = nt(grad_pre_ref[...], w_proj_ref[...])
    grad_gain = jnp.sum(grad_normed * hat, axis=0, keepdims=True)
    row_grads = (
        upstream.astype(F32) + norm_slope(grad_normed * gain, hat, inverse)
    ).astype(BF16)
    sent_ref[...] = nn(flag(placed == iota((slots, tokens), 0)), row_grads).astype(BF16)

    left_ref[0] = normed.T
    left_ref[1] = gated.T
    tail_ref[...] = gain_tail(
        jnp.concatenate(
            [grad_gain[:, k * LANES : (k + 1) * LANES] for k in range(width // LANES)], axis=0
        )
    )


def weights_kernel(left_ref, grad_pre_ref, upstream_ref, tail_ref, keep_ref, give_ref):
    width = upstream_ref.shape[1]
    inner = grad_pre_ref.shape[1] // 4
    half = keep_ref.shape[0] - 16
    core = lax.rem(lax.axis_index("dp"), 2)
    rows = width // 2
    blocks = (4 * inner + width) // LANES
    for out_ref, side in ((give_ref, 1 - core), (keep_ref, core)):
        out_ref[pl.ds(half, 16), :] = tail_ref[...]
        first = pl.multiple_of(side * rows, rows)
        left = left_ref[0, pl.ds(first, rows), :]
        value = nn(left, grad_pre_ref[...])
        for b in range(4 * inner // LANES):
            for p in range(4):
                out_ref[pl.ds((p * blocks + b) * STRIP, STRIP), :] = value[
                    p * STRIP : (p + 1) * STRIP, b * LANES : (b + 1) * LANES
                ].astype(BF16)
        value = nn(left_ref[1, pl.ds(first, rows), :], upstream_ref[...])
        for b in range(width // LANES):
            for p in range(4):
                at = (p * blocks + b + 4 * inner // LANES) * STRIP
                out_ref[pl.ds(at, STRIP), :] = value[
                    p * STRIP : (p + 1) * STRIP, b * LANES : (b + 1) * LANES
                ].astype(BF16)


def gain_tail(grad_gain):
    high = grad_gain.astype(BF16).astype(F32)
    low = grad_gain - high
    return jnp.concatenate([high, low, jnp.zeros((8, LANES), F32)], axis=0).astype(BF16)


def first_place():
    rank = lax.axis_index("dp")
    along_x = lax.rem(lax.axis_index("table"), XS)
    along_y = lax.div(rank, 2)
    core = lax.rem(rank, 2)
    return core, jnp.where(core == 0, along_x, along_y), jnp.where(core == 0, along_y, along_x)


def part_sum(refs, start, count):
    value = refs[0][pl.ds(start, count), :].astype(F32)
    for ref in refs[1:]:
        value = value + ref[pl.ds(start, count), :].astype(F32)
    return value


def tail_sum(refs, rows):
    tail = part_sum(refs, rows, 16)
    return gain_tail(tail[0:4] + tail[4:8])


def turned_merge_kernel(mine_ref, other_ref, *out_refs):
    refs = (mine_ref, other_ref)
    chunk = out_refs[0].shape[0] - 16
    ring = len(out_refs)
    tail = tail_sum(refs, ring * chunk)
    _, place, _ = first_place()
    for d in (1, 2, 3, 0):
        start = pl.multiple_of(lax.rem(place + d, ring) * chunk, chunk)
        out_refs[d][pl.ds(0, chunk), :] = part_sum(refs, start, chunk).astype(BF16)
        out_refs[d][pl.ds(chunk, 16), :] = tail


def narrow_merge_kernel(*refs):
    refs, out_ref = refs[:-1], refs[-1]
    pieces, size, _ = out_ref.shape
    chunk = size - 8
    tail = tail_sum(refs, pieces * chunk).astype(F32)[0:8]
    for p in range(0, pieces, 2):
        two = part_sum(refs, p * chunk, 2 * chunk)
        for k in range(2):
            piece = jnp.concatenate([two[k * chunk : (k + 1) * chunk], tail], axis=0)
            out_ref[p + k] = piece.astype(BF16)


def add_kernel(near_ref, passed_ref, after_ref, sum_ref):
    sum_ref[...] = (near_ref[...].astype(F32) + passed_ref[...].astype(F32)).astype(BF16)


def turn_kernel(in_ref, after_ref, spread_ref, gain_ref):
    total = jnp.sum(in_ref[...].astype(F32), axis=0)
    rows = spread_ref.shape[1]
    mine = total[0:rows].astype(BF16)
    for p in range(spread_ref.shape[0]):
        spread_ref[p] = mine
    gain = total[rows : rows + 4] + total[rows + 4 : rows + 8]
    scale = lax.rsqrt(jnp.sum(gain * gain) / gain.size + STEP_EPS)
    gain_ref[...] = gain * scale


def finish_kernel(*refs):
    own_ref, near_ref, far_ref = refs[:3]
    pieces = refs[3:-6]
    table_ref, proj_ref, out_ref, sum_ref, stage_ref, sems = refs[-6:]
    sum_ref[...] = (
        own_ref[...].astype(F32) + near_ref[...].astype(F32) + far_ref[...].astype(F32)
    )
    copies = [pltpu.make_async_copy(sum_ref, table_ref, sems.at[len(pieces), 0])]
    copies[0].start()
    split = proj_ref.shape[1]
    blocks = stage_ref.shape[2] // LANES
    ring = len(pieces) // 2
    core, mine, other = first_place()

    def strip(piece, b):
        return piece[pl.ds(b * STRIP, STRIP), :].astype(F32)

    proj_sum = jnp.zeros((8, LANES), F32)
    out_sum = jnp.zeros((8, LANES), F32)
    for piece in pieces:
        for b in range(blocks):
            value = strip(piece, b)
            part = jnp.sum((value * value).reshape(STRIP // 8, 8, LANES), axis=0)
            if b * LANES < split:
                proj_sum = proj_sum + part
            else:
                out_sum = out_sum + part
    proj_scale = lax.rsqrt(jnp.sum(proj_sum) / proj_ref.size + STEP_EPS)
    out_scale = lax.rsqrt(jnp.sum(out_sum) / out_ref.size + STEP_EPS)
    for i, piece in enumerate(pieces):
        for b in range(blocks):
            scale = proj_scale if b * LANES < split else out_scale
            stage_ref[i, :, pl.ds(b * LANES, LANES)] = (strip(piece, b) * scale).astype(BF16)
        side, place = (core, mine) if i < ring else (1 - core, other)
        spot = side * ring + lax.rem(place + (ring - i % ring), ring)
        rows = pl.ds(pl.multiple_of(spot * STRIP, STRIP), STRIP)
        for k, (first, count, ref) in enumerate(
            ((0, split, proj_ref), (split, out_ref.shape[1], out_ref))
        ):
            copy = pltpu.make_async_copy(
                stage_ref.at[i, :, pl.ds(first, count)], ref.at[rows, :], sems.at[i, k]
            )
            copy.start()
            copies.append(copy)
    for copy in copies:
        copy.wait()


def hold_kernel(*refs):
    pass


ZS, XS, YS = 8, 4, 4


def device(z, x, y, c):
    return (z * XS + x) * (2 * YS) + y * 2 + c


PLACES = [(z, x, y, c) for z in range(ZS) for x in range(XS) for y in range(YS) for c in range(2)]
CORE_PERM = [(device(z, x, y, c), device(z, x, y, 1 - c)) for z, x, y, c in PLACES]


def first_perm(d):
    return [
        (
            device(z, x, y, c),
            device(z, (x + d) % XS, y, c) if c == 0 else device(z, x, (y + d) % YS, c),
        )
        for z, x, y, c in PLACES
    ]


def ring_perm(step):
    return [
        (device(z, x, y, c), device(z, x, (y + (step if c == 0 else -step)) % YS, c))
        for z, x, y, c in PLACES
    ]


SECOND_GROUPS = [
    [device(z, x, y, 0) for y in range(YS) for z in range(ZS)] for x in range(XS)
] + [[device(z, x, y, 1) for x in range(XS) for z in range(ZS)] for y in range(YS)]


def swap(values, groups):
    return lax.all_to_all(
        values, BOTH, split_axis=0, concat_axis=0, tiled=True, axis_index_groups=groups
    )


def body(table_rows, item_shard, item_slot, seq_lengths, cotangent, w_proj, w_out, norm_gain):
    shards = lax.axis_size("table")
    tokens = item_slot.shape[1]
    width = table_rows.shape[1]
    inner = w_out.shape[0]
    capacity = 2 * tokens // shards
    slots = shards * capacity
    requests, placed = call(
        functools.partial(request_kernel, table_rows.shape[0]),
        [shape((shards, capacity), jnp.int32), shape((1, tokens), jnp.int32)],
        item_shard.reshape(1, tokens) * table_rows.shape[0] + item_slot,
        flops=4 * slots * width * table_rows.shape[0],
    )
    asked = lax.all_to_all(requests, "table", split_axis=0, concat_axis=0, tiled=True)
    (picked,) = call(
        pick_kernel,
        [shape((slots, width), BF16)],
        asked,
        table_rows,
        flops=2 * slots * width * table_rows.shape[0],
    )
    returned = lax.all_to_all(
        picked.reshape(shards, capacity, width), "table", split_axis=0, concat_axis=0, tiled=True
    ).reshape(slots, width)
    half = width * (4 * inner + width) // (2 * LANES)
    grad_half = shape((half + 16, LANES), BF16)
    layer_rows, sent, grad_pre, left, tail = call(
        layer_kernel,
        [
            shape((tokens, width), BF16),
            shape((slots, width), BF16),
            shape((tokens, 4 * inner), BF16),
            shape((2, width, tokens), BF16),
            shape((16, LANES), BF16),
        ],
        seq_lengths[0],
        returned,
        placed,
        cotangent[0],
        w_proj,
        w_out,
        norm_gain.reshape(1, width),
        specs=[SMEM] + [VMEM] * 6,
        flops=4 * tokens * width * (4 * inner + width),
        transcendentals=tokens * (4 * inner + HEADS * tokens),
        scratch=[
            pltpu.VMEM((tokens, 4 * inner), F32),
            pltpu.VMEM((tokens, 4 * inner), BF16),
        ],
    )
    keep, give = call(
        weights_kernel,
        [grad_half, grad_half],
        left,
        grad_pre,
        cotangent[0],
        tail,
        flops=2 * tokens * width * (4 * inner + width),
    )
    got = lax.all_to_all(
        sent.reshape(shards, capacity, width), "table", split_axis=0, concat_axis=0, tiled=True
    ).reshape(slots, width)
    rows = table_rows.shape[0] // (2 * YS)
    other = lax.ppermute(give, BOTH, CORE_PERM)
    parts = call(turned_merge_kernel, [shape((half // 4 + 16, LANES), BF16)] * 4, keep, other)
    parts = [parts[0]] + [lax.ppermute(parts[d], BOTH, first_perm(d)) for d in (1, 2, 3)]
    (grads,) = call(narrow_merge_kernel, [shape((32, half // 128 + 8, LANES), BF16)], *parts)
    own, near, two, far = call(
        dense_kernel,
        [shape((rows, width), BF16)] * YS,
        asked,
        lax.ppermute(asked, BOTH, CORE_PERM),
        got,
        lax.ppermute(got, BOTH, CORE_PERM),
        grads,
        specs=[VMEM] * 4 + [ANY],
        flops=2 * slots * width * table_rows.shape[0],
    )
    passed = lax.ppermute(two, BOTH, ring_perm(1))
    far = lax.ppermute(far, BOTH, ring_perm(-1))
    grads = swap(grads, SECOND_GROUPS)
    grads, step_gain = call(
        turn_kernel,
        [shape((32, half // 128, LANES), BF16), shape((width // LANES, LANES), F32)],
        grads,
        near,
        specs=[VMEM, ANY],
    )
    (near,) = call(
        add_kernel,
        [shape((rows, width), BF16)],
        near,
        passed,
        grads,
        specs=[VMEM, VMEM, ANY],
    )
    near_sum = near
    near = lax.ppermute(near_sum, BOTH, ring_perm(1))
    grads = swap(grads, SECOND_GROUPS).reshape(half // 4, LANES)
    (grads,) = call(
        hold_kernel,
        [shape(grads.shape, BF16)],
        grads,
        near_sum,
        specs=[ANY] * 2,
        out_specs=[ANY],
        aliases={0: 0},
    )
    mine = [grads] + [lax.ppermute(grads, BOTH, first_perm(d)) for d in (1, 2, 3)]
    (mine[1],) = call(
        hold_kernel,
        [shape(grads.shape, BF16)],
        mine[1],
        near,
        far,
        specs=[ANY] * 3,
        out_specs=[ANY],
        aliases={0: 0},
    )
    others = [lax.ppermute(piece, BOTH, CORE_PERM) for piece in mine]
    table_grad, step_proj, step_out = call(
        finish_kernel,
        [shape((rows, width), F32), shape(w_proj.shape, BF16), shape(w_out.shape, BF16)],
        own,
        near,
        far,
        *mine,
        *others,
        out_specs=[HBM, HBM, HBM],
        scratch=[
            pltpu.VMEM((rows, width), F32),
            pltpu.VMEM((8, STRIP, 4 * inner + width), BF16),
            pltpu.SemaphoreType.DMA((9, 2)),
        ],
    )
    return (layer_rows[None], table_grad, step_proj, step_out, step_gain.reshape(width))


def solution(mesh):
    placed = (
        P("table", None),
        P("dp", "table", None),
        P("dp", "table"),
        P("dp", "table", None),
        P("dp", "table", None),
        P(),
        P(),
        P(),
    )
    return jax.shard_map(
        body,
        mesh=mesh,
        in_specs=placed,
        out_specs=(P("dp", "table", None), P(("table", "dp"), None), P(), P(), P()),
        check_vma=False,
    )
```
